256 devices in a mesh: group: 8 (over z), dev: 32 (over y, x, core).
Axes of the slice: x: 4, y: 4, z: 8, core: 2. Of those that a mesh axis runs over, the one named last changes fastest.
Arguments:
- features: bfloat16 [1536, 64, 512], P(('group', 'dev')), may hold values from -6 to 6
- cotangent: bfloat16 [1536, 64, 512], P(('group', 'dev')), may hold values from -0.03125 to 0.03125
- first_weight: bfloat16 [64, 27, 64], replicated, may hold values from -0.15625 to 0.15625
- second_weight: bfloat16 [64, 27, 64], replicated, may hold values from -0.15625 to 0.15625
- counts: int32 [8, 32], replicated, may hold values from 0 to 6, as said below
- neighbours: int32 [1536, 26], P(('group', 'dev')), may hold values from -1 to 1535, as said below
Outputs:
- blocks_out: bfloat16 [1536, 64, 512], P(('group', 'dev'))
- first_grad: float32 [64, 27, 64], replicated
- second_grad: float32 [64, 27, 64], replicated
The draws below stay inside these ranges and needn't reach their ends.
Inputs may be any that keep to these rules, and one draw needn't show every extreme that they name: `counts`: slots 0 to count - 1 of a device hold its bricks. The bricks of group g form one layer of the scene, 64 of them, taken along a Morton curve of the layer and cut into consecutive ranges, device after device. In every group some device holds 6 bricks. A live brick's entries name live bricks only; free slots hold -1 in every direction. A brick of group g has neighbours only in groups g + dz. The relation is symmetric: if s names r in direction k, r names s in the opposite direction.
All inputs are finite; a program needn't handle non-finite values.
Results may differ from the reference program's by a relative error of at most 0.005.
Values may be sent and summed in bfloat16 or wider, within the bound.
A program may use at most 128 MiB of HBM per device.

```python
import jax
import jax.numpy as jnp
import numpy as np
from jax import lax

C = 64
VOXELS = 512
TAPS = 27
MEAN = 2
CAP = 6
SLOTS = 1536
N_GROUP = 8
N_DEV = 32


def split_bits(codes, parity, bit_total):
    total = jnp.zeros_like(codes)
    for index in range(bit_total):
        total = total + codes // 2 ** (2 * index + parity) % 2 * 2 ** index
    return total


def join_bits(coord_x, coord_y, horizontal_bits, y_bits):
    total = jnp.zeros_like(coord_x)
    for index in range(horizontal_bits):
        total = total + coord_x // 2 ** index % 2 * 2 ** (2 * index)
    for index in range(y_bits):
        total = total + coord_y // 2 ** index % 2 * 2 ** (2 * index + 1)
    return total


def scene_layout(key):
    per_group = N_DEV * MEAN
    cells = 2 * per_group
    bit_count = cells.bit_length() - 1
    horizontal_bits = (bit_count + 1) // 2
    y_bits = bit_count // 2
    pattern = jnp.asarray(np.array([3 * MEAN, 2 * MEAN, MEAN, MEAN, MEAN, 0, 0, 0] * (N_DEV // 8), dtype=np.int32))
    count_rows = []
    code_rows = []
    for group_id in range(N_GROUP):
        group_key = jax.random.fold_in(key, 1000 + group_id)
        count_key, cell_key = jax.random.split(group_key)
        count_rows.append(jax.random.permutation(count_key, pattern).astype(jnp.int32))
        picked = jax.random.permutation(cell_key, cells)[:per_group]
        code_rows.append(jnp.sort(picked).astype(jnp.int32))
    counts = jnp.stack(count_rows)
    codes = jnp.stack(code_rows)
    ends = jnp.cumsum(counts, axis=1)
    starts = ends - counts
    rank_ids = jnp.arange(per_group, dtype=jnp.int32)
    owners = jnp.sum((ends[:, None, :] <= rank_ids[None, :, None]).astype(jnp.int32), axis=2)
    within = rank_ids[None, :] - jnp.take_along_axis(starts, owners, axis=1)
    group_ids = jnp.arange(N_GROUP, dtype=jnp.int32)[:, None]
    slot_of_rank = ((group_ids * N_DEV + owners) * CAP + within).astype(jnp.int32)
    cell_slot = jnp.full((N_GROUP, cells), -1, jnp.int32).at[jnp.broadcast_to(group_ids, codes.shape), codes].set(slot_of_rank)
    slot_local = jnp.arange(CAP, dtype=jnp.int32)
    ranks = starts[:, :, None] + slot_local[None, None, :]
    alive = slot_local[None, None, :] < counts[:, :, None]
    safe_rank = jnp.minimum(ranks, per_group - 1)
    slot_codes = jnp.take_along_axis(codes, safe_rank.reshape(N_GROUP, -1), axis=1).reshape(N_GROUP, N_DEV, CAP)
    coord_x = split_bits(slot_codes, 0, horizontal_bits)
    coord_y = split_bits(slot_codes, 1, y_bits)
    layer = jnp.broadcast_to(jnp.arange(N_GROUP, dtype=jnp.int32)[:, None, None], slot_codes.shape)
    columns = []
    for step_z in (-1, 0, 1):
        for step_y in (-1, 0, 1):
            for step_x in (-1, 0, 1):
                if step_z == 0 and step_y == 0 and (step_x == 0):
                    continue
                near_x = coord_x + step_x
                near_y = coord_y + step_y
                near_layer = layer + step_z
                inside = alive & (near_x >= 0) & (near_x < 2 ** horizontal_bits) & (near_y >= 0) & (near_y < 2 ** y_bits)
                inside = inside & (near_layer >= 0) & (near_layer < N_GROUP)
                near_code = join_bits(jnp.clip(near_x, 0, 2 ** horizontal_bits - 1), jnp.clip(near_y, 0, 2 ** y_bits - 1), horizontal_bits, y_bits)
                found = cell_slot[jnp.clip(near_layer, 0, N_GROUP - 1), near_code]
                columns.append(jnp.where(inside, found, -1))
    neighbours = jnp.stack(columns, axis=-1).reshape(N_GROUP * N_DEV * CAP, 26).astype(jnp.int32)
    return (counts, neighbours)


def draw_counts(key, part):
    layout = scene_layout(key)
    return layout[0]


def draw_neighbours(key, part):
    layout = scene_layout(key)
    return layout[1]


def levels(stream_key, shape, cuts, least, top_value):
    level, own = 1.0, jax.random.fold_in(stream_key, 6)
    for dim, blocks in cuts:
        draws = jnp.exp(jax.random.uniform(jax.random.fold_in(own, dim), (blocks,), jnp.float32, least / len(cuts), top_value / len(cuts)))
        level = level * jnp.repeat(draws, shape[dim] // blocks).reshape([-1 if axis == dim else 1 for axis in range(len(shape))])
    return level


def centred(rng, extent, scale, reach, shards=(), kind=jnp.bfloat16):
    entries = scale * jax.random.normal(rng, extent, jnp.float32)
    if shards:
        entries = entries * levels(rng, extent, shards, -0.22, 0.18)
    return jnp.clip(entries, -reach, reach).astype(kind)


def setup_inputs(seed: int = 0) -> dict:
    streams_of = jax.random.split(jax.random.key(seed), 7)
    features = centred(streams_of[0], (SLOTS, C, VOXELS), 1.0, 6.0, ((0, 256),))
    cotangent = centred(streams_of[1], (SLOTS, C, VOXELS), 0.002, 0.03125, ((0, 256),))
    first_weight = centred(streams_of[2], (C, TAPS, C), (TAPS * C) ** -0.5, 0.15625)
    second_weight = centred(streams_of[3], (C, TAPS, C), (TAPS * C) ** -0.5, 0.15625)
    counts = draw_counts(jax.random.fold_in(streams_of[6], 71), 0)
    neighbours = draw_neighbours(jax.random.fold_in(streams_of[6], 71), 0)
    return {"features": features, "cotangent": cotangent, "first_weight": first_weight, "second_weight": second_weight, "counts": counts, "neighbours": neighbours}


def cube_tables():
    face_index = []
    for face_id in range(6):
        for outer in range(8):
            for inner in range(8):
                edge_value = 0 if face_id % 2 == 0 else 7
                if face_id < 2:
                    face_index.append(outer * 64 + inner * 8 + edge_value)
                elif face_id < 4:
                    face_index.append(outer * 64 + edge_value * 8 + inner)
                else:
                    face_index.append(edge_value * 64 + outer * 8 + inner)
    directions = []
    for step_z in (-1, 0, 1):
        for step_y in (-1, 0, 1):
            for step_x in (-1, 0, 1):
                if step_z != 0 or step_y != 0 or step_x != 0:
                    directions.append((step_z, step_y, step_x))
    halo_direction = []
    halo_column = []
    cube_order = []
    for placement_depth in range(-1, 9):
        for place_y in range(-1, 9):
            for place_x in range(-1, 9):
                if 0 <= placement_depth < 8 and 0 <= place_y < 8 and 0 <= place_x < 8:
                    cube_order.append(placement_depth * 64 + place_y * 8 + place_x)
                    continue
                step_z = -1 if placement_depth < 0 else (1 if placement_depth > 7 else 0)
                step_y = -1 if place_y < 0 else (1 if place_y > 7 else 0)
                step_x = -1 if place_x < 0 else (1 if place_x > 7 else 0)
                other_z = placement_depth - 8 * step_z
                other_y = place_y - 8 * step_y
                other_x = place_x - 8 * step_x
                if step_z != 0:
                    face_id = 4 if step_z == 1 else 5
                    within = other_y * 8 + other_x
                elif step_x != 0:
                    face_id = 0 if step_x == 1 else 1
                    within = other_z * 8 + other_y
                else:
                    face_id = 2 if step_y == 1 else 3
                    within = other_z * 8 + other_x
                halo_direction.append(directions.index((step_z, step_y, step_x)))
                halo_column.append(face_id * 64 + within)
                cube_order.append(512 + len(halo_column) - 1)
    return (np.array(face_index, np.int32), np.array(halo_direction, np.int32),
            np.array(halo_column, np.int32), np.array(cube_order, np.int32))


def build_cubes(bricks, neighbours):
    face_index, halo_direction, halo_column, cube_order = cube_tables()
    faces = jnp.take(bricks, jnp.asarray(face_index), axis=2)
    chosen = neighbours[:, jnp.asarray(halo_direction)]
    valid = chosen >= 0
    picked = faces[jnp.maximum(chosen, 0), :, jnp.asarray(halo_column)[None, :]]
    picked = jnp.where(valid[:, :, None], picked, jnp.zeros_like(picked))
    halo = jnp.transpose(picked, (0, 2, 1))
    cube = jnp.concatenate([bricks, halo], axis=2)
    return jnp.take(cube, jnp.asarray(cube_order), axis=2)


def stacked_taps(cube):
    channels = cube.shape[0]
    grid = cube.reshape(channels, 10, 10, 10)
    parts = []
    for offset_z in range(3):
        for offset_y in range(3):
            for offset_x in range(3):
                parts.append(grid[:, offset_z:offset_z + 8, offset_y:offset_y + 8, offset_x:offset_x + 8].reshape(channels, 512))
    return jnp.stack(parts).reshape(27 * channels, 512)


def convolve(brick_cubes, weight):
    flattened_weight = weight.reshape(weight.shape[0], -1)
    return lax.map(lambda cube: jnp.dot(flattened_weight, stacked_taps(cube), preferred_element_type=jnp.float32), brick_cubes)


def weight_gradient(gradient_list, brick_cubes):
    def accumulate(total, pair):
        grad_rows, cube = pair
        term = lax.dot_general(grad_rows, stacked_taps(cube), (((1,), (1,)), ((), ())), preferred_element_type=jnp.float32)
        return total + term, None

    start_total = jnp.zeros((gradient_list.shape[1], 27 * brick_cubes.shape[1]), jnp.float32)
    total, unused = lax.scan(accumulate, start_total, (gradient_list, brick_cubes))
    return total


def reference(features, cotangent, first_weight, second_weight, counts, neighbours):
    slot_ids = jnp.arange(features.shape[0], dtype=jnp.int32)
    live = (slot_ids % CAP) < counts.reshape(-1)[slot_ids // CAP]
    live_mask = live[:, None, None]
    x_cubes = build_cubes(features, neighbours)
    first = convolve(x_cubes, first_weight)
    hidden = jnp.where(live_mask, jnp.maximum(first, 0.0), 0.0).astype(jnp.bfloat16)
    h_cubes = build_cubes(hidden, neighbours)
    second = convolve(h_cubes, second_weight)
    blocks_out = jnp.where(live_mask, features.astype(jnp.float32) + second, 0.0).astype(jnp.bfloat16)
    upstream = jnp.where(live_mask, cotangent, jnp.zeros_like(cotangent))
    second_grad = weight_gradient(upstream, h_cubes)
    g_cubes = build_cubes(upstream, neighbours)
    flipped = jnp.transpose(second_weight[:, ::-1, :], (2, 1, 0))
    back = convolve(g_cubes, flipped)
    hidden_grad = jnp.where(hidden > 0, back, 0.0).astype(jnp.bfloat16)
    first_grad = weight_gradient(hidden_grad, x_cubes)
    return blocks_out, first_grad.reshape(first_weight.shape), second_grad.reshape(second_weight.shape)
```

```python
import functools

import jax
import jax.numpy as jnp
import numpy as np
from jax import lax
from jax.experimental import pallas as pl
from jax.experimental.pallas import tpu as pltpu
from jax.sharding import PartitionSpec as P

MESH = pl.DeviceIdType.MESH
F32 = jnp.float32
BF16 = jnp.bfloat16
N_Z, N_Y, N_X = 8, 4, 4
PAIRS = 3
DIRECTIONS = [
    (dz, dy, dx)
    for dz in (-1, 0, 1)
    for dy in (-1, 0, 1)
    for dx in (-1, 0, 1)
    if (dz, dy, dx) != (0, 0, 0)
]


def face_of(direction):
    dz, dy, dx = direction
    if dz != 0:
        return (0 if dz == 1 else 1), 2
    if dx != 0:
        return (0 if dx == 1 else 1), 0
    return (0 if dy == 1 else 1), 1


def place():
    d = lax.axis_index("dev")
    return lax.axis_index("group"), d // 8, (d // 2) % 4, d % 2


def device(g, y, x, c):
    return (g, (y * 4 + x) * 2 + c)


def greet(partners):
    barrier = pltpu.get_barrier_semaphore()
    for partner in partners:
        pl.semaphore_signal(barrier, inc=1, device_id=partner, device_id_type=MESH)
    pl.semaphore_wait(barrier, len(partners))


def write_faces(value, scratch, outs, field, fields):
    scratch[...] = value
    cube = value.reshape(8, 8, 8, 128)
    for half, edge in ((0, 0), (1, 7)):
        out = outs[half]
        out[0, 0 * fields + field] = scratch[pl.ds(edge, 64, stride=8), :].astype(BF16)
        out[0, 1 * fields + field] = cube[:, edge].reshape(64, 128).astype(BF16)
        out[0, 2 * fields + field] = value[edge * 64:edge * 64 + 64].astype(BF16)


def live_lanes(count_ref, pair):
    lane = lax.broadcasted_iota(jnp.int32, (1, 128), 1)
    slot = 2 * pair + (lane >= 64).astype(jnp.int32)
    return slot < count_ref[0]


def pack_kernel(count_ref, f_ref, c_ref, x_out, g_out, fa_out, fb_out, scratch):
    pair = pl.program_id(0)
    xt = f_ref[0].astype(F32).T
    x_out[0] = xt.astype(BF16)
    write_faces(xt, scratch, (fa_out, fb_out), 0, 2)
    gt = jnp.where(live_lanes(count_ref, pair), c_ref[0].astype(F32).T, 0.0)
    g_out[0] = gt.astype(BF16)
    write_faces(gt, scratch, (fa_out, fb_out), 1, 2)


def pack(count, features, cotangent):
    blk = lambda *shape: pl.BlockSpec((1,) + shape, lambda p: (p,) + (0,) * len(shape))
    return pl.pallas_call(
        pack_kernel,
        grid=(PAIRS,),
        in_specs=[pl.BlockSpec(memory_space=pltpu.SMEM), blk(128, 512), blk(128, 512)],
        out_specs=[blk(512, 128), blk(512, 128), blk(6, 64, 128), blk(6, 64, 128)],
        out_shape=[
            jax.ShapeDtypeStruct((PAIRS, 512, 128), BF16),
            jax.ShapeDtypeStruct((PAIRS, 512, 128), BF16),
            jax.ShapeDtypeStruct((PAIRS, 6, 64, 128), BF16),
            jax.ShapeDtypeStruct((PAIRS, 6, 64, 128), BF16),
        ],
        scratch_shapes=[pltpu.VMEM((512, 128), F32)],
    )(count, features, cotangent)


def gather_kernel(fields, pos_ref, fa_ref, fb_ref, h_ref, buf_a, buf_b, send, recv):
    g, y, x, c = place()
    bufs, sources = (buf_a, buf_b), (fa_ref, fb_ref)

    def moved(axis, step):
        if axis == "x":
            return device(g, y, (x + step + N_X) % N_X, c)
        return device(g, (y + step + N_Y) % N_Y, x, c)

    below, above = device((g + N_Z - 1) % N_Z, y, x, c), device((g + 1) % N_Z, y, x, c)
    sibling = device(g, y, x, 1 - c)
    greet(
        [below, above, sibling]
        + [moved(axis, step) for axis in ("x", "y") for step in (1, -1)]
    )

    rings = (("x", "y"), ("y", "x"))
    mine = ((x, y), (y, x))

    def block(half, first):
        second = mine[half][1]
        return pl.ds(((c * 4 + second) * 4 + first) * 3, 3)

    def row(half, second):
        return pl.ds((c * 4 + second) * 12, 12)

    started = []

    def copy(half, number, src, dst, target):
        made = pltpu.make_async_remote_copy(
            src_ref=src,
            dst_ref=dst,
            send_sem=send.at[half, number],
            recv_sem=recv.at[half, number],
            device_id=target,
            device_id_type=MESH,
        )
        made.start()
        started.append(made)
        return made

    lower, upper = pl.ds(0, 32), pl.ds(32, 32)
    faces = 3 * fields
    plane = pl.ds(2 * fields, fields)
    sides = pl.ds(0, 2 * fields)
    zs, m = [], [dict(), dict()]
    for half in range(2):
        own = block(half, mine[half][0])
        zs.append(
            copy(
                half,
                0,
                sources[half].at[:, plane],
                bufs[half].at[own, plane],
                below if half == 0 else above,
            )
        )
        bufs[half][own, 0:2 * fields] = sources[half][:, 0:2 * fields]
        bufs[half][96:97] = jnp.zeros((1, faces, 64, 128), BF16)
    for half in range(2):
        own = block(half, mine[half][0])
        zs[half].wait_recv()
        for number, step in ((1, 1), (2, -1)):
            m[half][number] = copy(
                half, number, bufs[half].at[own], bufs[half].at[own],
                moved(rings[half][0], step),
            )
    for number, step, rows in ((3, 1, lower), (4, -1, upper)):
        for half in range(2):
            first = mine[half][0]
            m[half][number - 2].wait_recv()
            came = block(half, (first - step + 4) % 4)
            part = bufs[half].at[came, :, rows]
            m[half][number] = copy(half, number, part, part, moved(rings[half][0], step))
    for half in range(2):
        m[half][3].wait_recv()
        m[half][4].wait_recv()
        line = bufs[half].at[row(half, mine[half][1])]
        for number, step in ((5, 1), (6, -1)):
            m[half][number] = copy(half, number, line, line, moved(rings[half][1], step))
        m[half][9] = copy(half, 9, line, line, sibling)
    for number, step, rows in ((7, 1, lower), (8, -1, upper)):
        for half in range(2):
            second = mine[half][1]
            m[half][number - 2].wait_recv()
            came = row(half, (second - step + 4) % 4)
            part = bufs[half].at[came, :, rows]
            m[half][number] = copy(half, number, part, part, moved(rings[half][1], step))
            line = bufs[half].at[came]
            m[half][number + 3] = copy(half, number + 3, line, line, sibling)
    for number, rows in ((7, lower), (8, upper)):
        for half in range(2):
            m[half][number].wait_recv()
            part = bufs[half].at[row(half, (mine[half][1] + 2) % 4), :, rows]
            m[half][number + 5] = copy(half, number + 5, part, part, sibling)
    for half in range(2):
        for number in range(9, 14):
            m[half][number].wait_recv()
    for made in started:
        made.wait_send()

    def per_slot(slot, carry):
        for k, direction in enumerate(DIRECTIONS):
            half, face = face_of(direction)
            at = pos_ref[slot, k]
            for field in range(fields):
                h_ref[field, slot, k] = bufs[half][at, face * fields + field]
        return carry

    lax.fori_loop(0, 6, per_slot, 0)


def gather(fields, collective_id, pos, fa, fb):
    size = fields * 3 * 64 * 128 * 2 * 97 * 2
    return pl.pallas_call(
        functools.partial(gather_kernel, fields),
        in_specs=[
            pl.BlockSpec(memory_space=pltpu.SMEM),
            pl.BlockSpec(memory_space=pltpu.VMEM),
            pl.BlockSpec(memory_space=pltpu.VMEM),
        ],
        out_specs=pl.BlockSpec(memory_space=pltpu.VMEM),
        out_shape=jax.ShapeDtypeStruct((fields, 6, 26, 64, 128), BF16),
        scratch_shapes=[
            pltpu.VMEM((97, 3 * fields, 64, 128), BF16),
            pltpu.VMEM((97, 3 * fields, 64, 128), BF16),
            pltpu.SemaphoreType.DMA((2, 15)),
            pltpu.SemaphoreType.DMA((2, 15)),
        ],
        compiler_params=pltpu.CompilerParams(
            collective_id=collective_id,
            has_side_effects=True,
            vmem_limit_bytes=size + 16 * 2**20,
        ),
    )(pos, fa, fb)


def build_cube(cube, own, h_ref, par_ref, pair):
    low = lax.broadcasted_iota(jnp.int32, (1, 128), 1) < 64
    cube[1:9, 1:9, 8:16, :] = own.reshape(8, 8, 8, 128)
    for k, (dz, dy, dx) in enumerate(DIRECTIONS):
        if dz != 0 and dy != 0:
            start, count = (0, 16) if dy == 1 else (48, 16)
        else:
            start, count = 0, 64
        picked = []
        for s in range(2):
            value = h_ref[0, s, k, start:start + count].astype(F32)
            turned = pltpu.roll(value, 64, 1)
            picked.append(jnp.where(par_ref[2 * pair + s, k] == s, value, turned))
        piece = jnp.where(low, picked[0], picked[1])
        if count == 16:
            piece = piece[0:8] if dy == 1 else piece[8:16]
        zz = {-1: 0, 1: 9}.get(dz)
        yy = {-1: 0, 1: 9}.get(dy)
        if dx == 0:
            if dz == 0:
                cube[1:9, yy, 8:16, :] = piece.reshape(8, 8, 128)
            elif dy == 0:
                cube[zz, 1:9, 8:16, :] = piece.reshape(8, 8, 128)
            else:
                cube[zz, yy, 8:16, :] = piece
            continue
        sub = 7 if dx == -1 else 16
        edge_x = 7 if dx == -1 else 0
        edge_y = 7 if dy == -1 else 0
        if dz == 0 and dy == 0:
            rows = [(z + 1, q + 1, z * 8 + q) for z in range(8) for q in range(8)]
        elif dz == 0:
            rows = [(z + 1, yy, z * 8 + edge_y) for z in range(8)]
        elif dy == 0:
            rows = [(zz, q + 1, q * 8 + edge_x) for q in range(8)]
        else:
            rows = [(zz, yy, edge_x)]
        for a, b, r in rows:
            cube[a, b, sub:sub + 1, :] = piece[r:r + 1]


def stack_taps(cube, taps):
    for ty in range(3):
        for tx in range(3):
            part = cube[:, ty:ty + 8, 7 + tx:15 + tx, :].reshape(640, 128)
            column = (ty * 3 + tx) * 128
            taps[:, column:column + 128] = part.astype(BF16)


def convolve(taps, w_ref):
    wide = jnp.dot(taps[...], w_ref[...], preferred_element_type=F32)
    return wide[0:512, 0:128] + wide[64:576, 128:256] + wide[128:640, 256:384]


def spread(wide_g, value):
    for tz in range(3):
        wide_g[tz * 64:tz * 64 + 512, tz * 128:tz * 128 + 128] = value


def clear_spread(wide_g):
    wide_g[...] = jnp.zeros((640, 384), BF16)


def outer(wide_g, taps):
    return lax.dot_general(
        wide_g[...], taps[...], (((0,), (0,)), ((), ())), preferred_element_type=F32
    )


def first_kernel(count_ref, par_ref, x_ref, g_ref, hx_ref, hg_ref, w_ref, v_ref,
                 h_out, fa_out, fb_out, m_out, cube, taps, taps_g, wide_g, scratch):
    pair = pl.program_id(0)
    build_cube(cube, x_ref[0].astype(F32), hx_ref, par_ref, pair)
    stack_taps(cube, taps)
    first = convolve(taps, w_ref)
    hidden = jnp.where(live_lanes(count_ref, pair), jnp.maximum(first, 0.0), 0.0)
    hidden = hidden.astype(BF16).astype(F32)
    h_out[0] = hidden.astype(BF16)
    write_faces(hidden, scratch, (fa_out, fb_out), 0, 1)
    build_cube(cube, g_ref[0].astype(F32), hg_ref, par_ref, pair)
    stack_taps(cube, taps_g)
    back = convolve(taps_g, v_ref)
    hidden_grad = jnp.where(scratch[...] > 0, back, 0.0).astype(BF16)

    @pl.when(pair == 0)
    def _():
        clear_spread(wide_g)
        m_out[...] = jnp.zeros_like(m_out)

    spread(wide_g, hidden_grad)
    m_out[...] += outer(wide_g, taps)


def blocked(*shape):
    return pl.BlockSpec((1,) + shape, lambda p: (p,) + (0,) * len(shape))


def fixed(*shape):
    return pl.BlockSpec(shape, lambda p: (0,) * len(shape))


def halo_spec(field):
    return pl.BlockSpec((1, 2, 26, 64, 128), lambda p: (field, p, 0, 0, 0))


def first_part(count, parity, xt, gt, halos, w, v):
    smem = pl.BlockSpec(memory_space=pltpu.SMEM)
    return pl.pallas_call(
        first_kernel,
        grid=(PAIRS,),
        in_specs=[smem, smem, blocked(512, 128), blocked(512, 128), halo_spec(0),
                  halo_spec(1), fixed(1152, 384), fixed(1152, 384)],
        out_specs=[blocked(512, 128), blocked(3, 64, 128), blocked(3, 64, 128),
                   fixed(384, 1152)],
        out_shape=[
            jax.ShapeDtypeStruct((PAIRS, 512, 128), BF16),
            jax.ShapeDtypeStruct((PAIRS, 3, 64, 128), BF16),
            jax.ShapeDtypeStruct((PAIRS, 3, 64, 128), BF16),
            jax.ShapeDtypeStruct((384, 1152), F32),
        ],
        scratch_shapes=[
            pltpu.VMEM((10, 10, 24, 128), F32),
            pltpu.VMEM((640, 1152), BF16),
            pltpu.VMEM((640, 1152), BF16),
            pltpu.VMEM((640, 384), BF16),
            pltpu.VMEM((512, 128), F32),
        ],
        compiler_params=pltpu.CompilerParams(vmem_limit_bytes=40 * 2**20),
    )(count, parity, xt, gt, halos, halos, w, v)


def second_kernel(count_ref, par_ref, f_ref, h_ref, g_ref, hh_ref, w_ref, m1_ref,
                  o_out, p_out, cube, taps, wide_g, total):
    pair = pl.program_id(0)
    build_cube(cube, h_ref[0].astype(F32), hh_ref, par_ref, pair)
    stack_taps(cube, taps)
    second = convolve(taps, w_ref)
    slot = 2 * pair + (lax.broadcasted_iota(jnp.int32, (128, 1), 0) >= 64).astype(jnp.int32)
    result = f_ref[0].astype(F32) + second.T
    o_out[0] = jnp.where(slot < count_ref[0], result, 0.0).astype(BF16)

    @pl.when(pair == 0)
    def _():
        clear_spread(wide_g)
        total[...] = jnp.zeros_like(total)

    spread(wide_g, g_ref[0])
    total[...] += outer(wide_g, taps)

    @pl.when(pair == PAIRS - 1)
    def _():
        low = lax.broadcasted_iota(jnp.int32, (1, 128), 1) < 64
        for q in range(9):
            for tz in range(3):
                even, odd = pl.ds(tz * 128, 64), pl.ds(tz * 128 + 64, 64)
                lanes = pl.ds(q * 128, 128)
                one = m1_ref[even, lanes] + pltpu.roll(m1_ref[odd, lanes], 64, 1)
                two = pltpu.roll(total[even, lanes], 64, 1) + total[odd, lanes]
                p_out[pl.ds((q * 3 + tz) * 64, 64), :] = jnp.where(low, one, two)
        p_out[1728:2048, :] = jnp.zeros((320, 128), F32)


def second_part(count, parity, features, ht, gt, halos, v, m1):
    smem = pl.BlockSpec(memory_space=pltpu.SMEM)
    return pl.pallas_call(
        second_kernel,
        grid=(PAIRS,),
        in_specs=[smem, smem, blocked(128, 512), blocked(512, 128), blocked(512, 128),
                  halo_spec(0), fixed(1152, 384), fixed(384, 1152)],
        out_specs=[blocked(128, 512), fixed(2048, 128)],
        out_shape=[
            jax.ShapeDtypeStruct((PAIRS, 128, 512), BF16),
            jax.ShapeDtypeStruct((2048, 128), F32),
        ],
        scratch_shapes=[
            pltpu.VMEM((10, 10, 24, 128), F32),
            pltpu.VMEM((640, 1152), BF16),
            pltpu.VMEM((640, 384), BF16),
            pltpu.VMEM((384, 1152), F32),
        ],
        compiler_params=pltpu.CompilerParams(vmem_limit_bytes=40 * 2**20),
    )(count, parity, features, ht, gt, halos, v, m1)


def reduce_kernel(p_ref, out_ref, r1, a1, r2, a2, r3, r4, whole, send, recv):
    g, y, x, c = place()
    sibling = device(g, y, x, 1 - c)
    xs = [device(g, y, (x + k) % N_X, c) for k in range(1, N_X)]
    ys = [device(g, (y + k) % N_Y, x, c) for k in range(1, N_Y)]
    zs = [device((g + k) % N_Z, y, x, c) for k in range(1, N_Z)]
    greet([sibling] + xs + ys + zs)
    used = [0]

    def copy(src, dst, target):
        number = used[0]
        used[0] += 1
        made = pltpu.make_async_remote_copy(
            src_ref=src, dst_ref=dst, send_sem=send.at[number], recv_sem=recv.at[number],
            device_id=target, device_id_type=MESH,
        )
        made.start()
        return made

    copy(p_ref.at[pl.ds((1 - c) * 1024, 1024)], r1, sibling).wait()
    a1[...] = (p_ref[pl.ds(c * 1024, 1024)] + r1[...]).astype(BF16)

    made = [
        copy(a1.at[pl.ds(((x + k) % N_X) * 256, 256)], r2.at[k - 1], xs[k - 1])
        for k in range(1, N_X)
    ]
    for one in made:
        one.wait()
    part = a1[pl.ds(x * 256, 256)].astype(F32)
    for k in range(3):
        part = part + r2[k].astype(F32)
    a2[...] = part

    made = [
        copy(a2.at[pl.ds(((y + k) % N_Y) * 64, 64)], r3.at[k - 1], ys[k - 1])
        for k in range(1, N_Y)
    ]
    for one in made:
        one.wait()
    part = a2[pl.ds(y * 64, 64)]
    for k in range(3):
        part = part + r3[k]
    r4[g] = part.astype(BF16)

    made = [copy(r4.at[g], r4.at[g], zs[k - 1]) for k in range(1, N_Z)]
    for one in made:
        one.wait()
    part = r4[0].astype(F32)
    for k in range(1, N_Z):
        part = part + r4[k].astype(F32)
    start = ((c * 4 + x) * 4 + y) * 64
    whole[pl.ds(start, 64)] = part.astype(BF16)

    for rows, targets in (
        (pl.ds(start, 64), ys),
        (pl.ds((c * 4 + x) * 256, 256), xs),
        (pl.ds(c * 1024, 1024), [sibling]),
    ):
        made = [copy(whole.at[rows], whole.at[rows], target) for target in targets]
        for one in made:
            one.wait()
    out_ref[...] = whole[...]


def reduce_all(p):
    return pl.pallas_call(
        reduce_kernel,
        in_specs=[pl.BlockSpec(memory_space=pltpu.VMEM)],
        out_specs=pl.BlockSpec(memory_space=pltpu.VMEM),
        out_shape=jax.ShapeDtypeStruct((2048, 128), BF16),
        scratch_shapes=[
            pltpu.VMEM((1024, 128), F32),
            pltpu.VMEM((1024, 128), BF16),
            pltpu.VMEM((3, 256, 128), BF16),
            pltpu.VMEM((256, 128), F32),
            pltpu.VMEM((3, 64, 128), F32),
            pltpu.VMEM((N_Z, 64, 128), BF16),
            pltpu.VMEM((2048, 128), BF16),
            pltpu.SemaphoreType.DMA((24,)),
            pltpu.SemaphoreType.DMA((24,)),
        ],
        compiler_params=pltpu.CompilerParams(
            collective_id=2, has_side_effects=True, vmem_limit_bytes=16 * 2**20
        ),
    )(p)


def block_weight(w):
    turned = jnp.transpose(w, (2, 3, 4, 1, 0))[:, :, None, :, :, None, :]
    same = jnp.eye(2, dtype=w.dtype)[None, None, :, None, None, :, None]
    return (turned * same).reshape(1152, 384)


def halo_places(neighbours):
    halves = jnp.asarray(np.array([face_of(d)[0] for d in DIRECTIONS], np.int32))[None, :]
    dev = neighbours // 6 % 32
    y, x, c = dev // 8, dev // 2 % 4, dev % 2
    first = jnp.where(halves == 0, x, y)
    second = jnp.where(halves == 0, y, x)
    pos = ((c * 4 + second) * 4 + first) * 3 + neighbours % 6 // 2
    return jnp.where(neighbours >= 0, pos, 96).astype(jnp.int32), neighbours % 2


def per_device(features, cotangent, first_weight, second_weight, counts, neighbours):
    count = counts[lax.axis_index("group"), lax.axis_index("dev")].reshape(1)
    pos, parity = halo_places(neighbours)
    w1 = first_weight.reshape(64, 3, 3, 3, 64)
    w2 = second_weight.reshape(64, 3, 3, 3, 64)
    wide1, wide2 = block_weight(w1), block_weight(w2)
    wide_back = block_weight(jnp.transpose(w2[:, ::-1, ::-1, ::-1, :], (4, 1, 2, 3, 0)))
    feats = features.reshape(PAIRS, 128, 512)
    xt, gt, fa, fb = pack(count, feats, cotangent.reshape(PAIRS, 128, 512))
    halos = gather(2, 0, pos, fa, fb)
    ht, ha, hb, m1 = first_part(count, parity, xt, gt, halos, wide1, wide_back)
    halos_h = gather(1, 1, pos, ha, hb)
    out, p = second_part(count, parity, feats, ht, gt, halos_h, wide2, m1)
    total = reduce_all(p)
    total = total[:1728].reshape(3, 3, 3, 64, 2, 64)
    grads = jnp.transpose(total, (4, 3, 2, 0, 1, 5)).reshape(2, 64, 27, 64).astype(F32)
    return out.reshape(6, 64, 512), grads[0], grads[1]


def solution(mesh):
    placed = (
        P(("group", "dev"), None, None),
        P(("group", "dev"), None, None),
        P(),
        P(),
        P(),
        P(("group", "dev"), None),
    )
    return jax.shard_map(
        per_device,
        mesh=mesh,
        in_specs=placed,
        out_specs=(P(("group", "dev"), None, None), P(), P()),
        check_vma=False,
    )
```

```python
import functools

import jax
import jax.numpy as jnp
import numpy as np
from jax import lax
from jax.experimental import pallas as pl
from jax.experimental.pallas import tpu as pltpu
from jax.sharding import PartitionSpec as P

MESH = pl.DeviceIdType.MESH
F32 = jnp.float32
BF16 = jnp.bfloat16
N_Z, N_Y, N_X = 8, 4, 4
PAIRS = 3
DIRECTIONS = [
    (dz, dy, dx)
    for dz in (-1, 0, 1)
    for dy in (-1, 0, 1)
    for dx in (-1, 0, 1)
    if (dz, dy, dx) != (0, 0, 0)
]


def face_of(direction):
    dz, dy, dx = direction
    if dz != 0:
        return (0 if dz == 1 else 1), 2
    if dx != 0:
        return (0 if dx == 1 else 1), 0
    return (0 if dy == 1 else 1), 1


def place():
    d = lax.axis_index("dev")
    return lax.axis_index("group"), d // 8, (d // 2) % 4, d % 2


def device(g, y, x, c):
    return (g, (y * 4 + x) * 2 + c)


def greet(partners):
    barrier = pltpu.get_barrier_semaphore()
    for partner in partners:
        pl.semaphore_signal(barrier, inc=1, device_id=partner, device_id_type=MESH)
    pl.semaphore_wait(barrier, len(partners))


def write_faces(value, scratch, outs, field, fields):
    scratch[...] = value
    cube = value.reshape(8, 8, 8, 128)
    for half, edge in ((0, 0), (1, 7)):
        out = outs[half]
        out[0, 0 * fields + field] = scratch[pl.ds(edge, 64, stride=8), :].astype(BF16)
        out[0, 1 * fields + field] = cube[:, edge].reshape(64, 128).astype(BF16)
        out[0, 2 * fields + field] = value[edge * 64:edge * 64 + 64].astype(BF16)


def own_count(count_ref):
    return count_ref[lax.axis_index("group"), lax.axis_index("dev")]


def live_lanes(count_ref, pair):
    lane = lax.broadcasted_iota(jnp.int32, (1, 128), 1)
    slot = 2 * pair + (lane >= 64).astype(jnp.int32)
    return slot < own_count(count_ref)


def pack_kernel(count_ref, f_ref, c_ref, x_out, g_out, fa_out, fb_out, scratch):
    pair = pl.program_id(0)
    xt = f_ref[0].astype(F32).T
    x_out[0] = xt.astype(BF16)
    write_faces(xt, scratch, (fa_out, fb_out), 0, 2)
    gt = jnp.where(live_lanes(count_ref, pair), c_ref[0].astype(F32).T, 0.0)
    g_out[0] = gt.astype(BF16)
    write_faces(gt, scratch, (fa_out, fb_out), 1, 2)


def pack(count, features, cotangent):
    blk = lambda *shape: pl.BlockSpec((1,) + shape, lambda p: (p,) + (0,) * len(shape))
    return pl.pallas_call(
        pack_kernel,
        grid=(PAIRS,),
        in_specs=[pl.BlockSpec(memory_space=pltpu.SMEM), blk(128, 512), blk(128, 512)],
        out_specs=[blk(512, 128), blk(512, 128), blk(6, 64, 128), blk(6, 64, 128)],
        out_shape=[
            jax.ShapeDtypeStruct((PAIRS, 512, 128), BF16),
            jax.ShapeDtypeStruct((PAIRS, 512, 128), BF16),
            jax.ShapeDtypeStruct((PAIRS, 6, 64, 128), BF16),
            jax.ShapeDtypeStruct((PAIRS, 6, 64, 128), BF16),
        ],
        scratch_shapes=[pltpu.VMEM((512, 128), F32)],
    )(count, features, cotangent)


def gather_kernel(fields, pos_ref, fa_ref, fb_ref, h_ref, buf_a, buf_b, send, recv):
    g, y, x, c = place()
    bufs, sources = (buf_a, buf_b), (fa_ref, fb_ref)

    def moved(axis, step):
        if axis == "x":
            return device(g, y, (x + step + N_X) % N_X, c)
        return device(g, (y + step + N_Y) % N_Y, x, c)

    below, above = device((g + N_Z - 1) % N_Z, y, x, c), device((g + 1) % N_Z, y, x, c)
    sibling = device(g, y, x, 1 - c)
    greet(
        [below, above, sibling]
        + [moved(axis, step) for axis in ("x", "y") for step in (1, -1)]
    )

    rings = (("x", "y"), ("y", "x"))
    mine = ((x, y), (y, x))

    def block(half, first):
        second = mine[half][1]
        return pl.ds(((c * 4 + second) * 4 + first) * 3, 3)

    def row(half, second):
        return pl.ds((c * 4 + second) * 12, 12)

    started = []

    def copy(half, number, src, dst, target):
        made = pltpu.make_async_remote_copy(
            src_ref=src,
            dst_ref=dst,
            send_sem=send.at[half, number],
            recv_sem=recv.at[half, number],
            device_id=target,
            device_id_type=MESH,
        )
        made.start()
        started.append(made)
        return made

    lower, upper = pl.ds(0, 32), pl.ds(32, 32)
    faces = 3 * fields
    plane = pl.ds(2 * fields, fields)
    sides = pl.ds(0, 2 * fields)
    zs, m = [], [dict(), dict()]
    for half in range(2):
        own = block(half, mine[half][0])
        zs.append(
            copy(
                half,
                0,
                sources[half].at[:, plane],
                bufs[half].at[own, plane],
                below if half == 0 else above,
            )
        )
        bufs[half][own, 0:2 * fields] = sources[half][:, 0:2 * fields]
        bufs[half][96:97] = jnp.zeros((1, faces, 64, 128), BF16)
    for half in range(2):
        own = block(half, mine[half][0])
        zs[half].wait_recv()
        for number, step in ((1, 1), (2, -1)):
            m[half][number] = copy(
                half, number, bufs[half].at[own], bufs[half].at[own],
                moved(rings[half][0], step),
            )
    for number, step, rows in ((3, 1, lower), (4, -1, upper)):
        for half in range(2):
            first = mine[half][0]
            m[half][number - 2].wait_recv()
            came = block(half, (first - step + 4) % 4)
            part = bufs[half].at[came, :, rows]
            m[half][number] = copy(half, number, part, part, moved(rings[half][0], step))
    for half in range(2):
        m[half][3].wait_recv()
        m[half][4].wait_recv()
        line = bufs[half].at[row(half, mine[half][1])]
        for number, step in ((5, 1), (6, -1)):
            m[half][number] = copy(half, number, line, line, moved(rings[half][1], step))
        m[half][9] = copy(half, 9, line, line, sibling)
    for number, step, rows in ((7, 1, lower), (8, -1, upper)):
        for half in range(2):
            second = mine[half][1]
            m[half][number - 2].wait_recv()
            came = row(half, (second - step + 4) % 4)
            part = bufs[half].at[came, :, rows]
            m[half][number] = copy(half, number, part, part, moved(rings[half][1], step))
            line = bufs[half].at[came]
            m[half][number + 3] = copy(half, number + 3, line, line, sibling)
    for number, rows in ((7, lower), (8, upper)):
        for half in range(2):
            m[half][number].wait_recv()
            part = bufs[half].at[row(half, (mine[half][1] + 2) % 4), :, rows]
            m[half][number + 5] = copy(half, number + 5, part, part, sibling)
    for half in range(2):
        for number in range(9, 14):
            m[half][number].wait_recv()
    for made in started:
        made.wait_send()

    def per_slot(slot, carry):
        for k, direction in enumerate(DIRECTIONS):
            half, face = face_of(direction)
            at = pos_ref[slot, k]
            for field in range(fields):
                h_ref[field, slot, k] = bufs[half][at, face * fields + field]
        return carry

    lax.fori_loop(0, 6, per_slot, 0)


def gather(fields, collective_id, pos, fa, fb):
    size = fields * 3 * 64 * 128 * 2 * 97 * 2
    return pl.pallas_call(
        functools.partial(gather_kernel, fields),
        in_specs=[
            pl.BlockSpec(memory_space=pltpu.SMEM),
            pl.BlockSpec(memory_space=pltpu.VMEM),
            pl.BlockSpec(memory_space=pltpu.VMEM),
        ],
        out_specs=pl.BlockSpec(memory_space=pltpu.VMEM),
        out_shape=jax.ShapeDtypeStruct((fields, 6, 26, 64, 128), BF16),
        scratch_shapes=[
            pltpu.VMEM((97, 3 * fields, 64, 128), BF16),
            pltpu.VMEM((97, 3 * fields, 64, 128), BF16),
            pltpu.SemaphoreType.DMA((2, 15)),
            pltpu.SemaphoreType.DMA((2, 15)),
        ],
        compiler_params=pltpu.CompilerParams(
            collective_id=collective_id,
            has_side_effects=True,
            vmem_limit_bytes=size + 16 * 2**20,
        ),
    )(pos, fa, fb)


def build_cube(cube, own, h_ref, par_ref, pair):
    low = lax.broadcasted_iota(jnp.int32, (1, 128), 1) < 64
    cube[1:9, 1:9, 8:16, :] = own.reshape(8, 8, 8, 128)
    for k, (dz, dy, dx) in enumerate(DIRECTIONS):
        if dz != 0 and dy != 0:
            start, count = (0, 16) if dy == 1 else (48, 16)
        else:
            start, count = 0, 64
        picked = []
        for s in range(2):
            value = h_ref[0, s, k, start:start + count].astype(F32)
            turned = pltpu.roll(value, 64, 1)
            picked.append(jnp.where(par_ref[2 * pair + s, k] == s, value, turned))
        piece = jnp.where(low, picked[0], picked[1])
        if count == 16:
            piece = piece[0:8] if dy == 1 else piece[8:16]
        zz = {-1: 0, 1: 9}.get(dz)
        yy = {-1: 0, 1: 9}.get(dy)
        if dx == 0:
            if dz == 0:
                cube[1:9, yy, 8:16, :] = piece.reshape(8, 8, 128)
            elif dy == 0:
                cube[zz, 1:9, 8:16, :] = piece.reshape(8, 8, 128)
            else:
                cube[zz, yy, 8:16, :] = piece
            continue
        sub = 7 if dx == -1 else 16
        edge_x = 7 if dx == -1 else 0
        edge_y = 7 if dy == -1 else 0
        if dz == 0 and dy == 0:
            rows = [(z + 1, q + 1, z * 8 + q) for z in range(8) for q in range(8)]
        elif dz == 0:
            rows = [(z + 1, yy, z * 8 + edge_y) for z in range(8)]
        elif dy == 0:
            rows = [(zz, q + 1, q * 8 + edge_x) for q in range(8)]
        else:
            rows = [(zz, yy, edge_x)]
        for a, b, r in rows:
            cube[a, b, sub:sub + 1, :] = piece[r:r + 1]


def stack_taps(cube, taps):
    for ty in range(3):
        for tx in range(3):
            part = cube[:, ty:ty + 8, 7 + tx:15 + tx, :].reshape(640, 128)
            column = (ty * 3 + tx) * 128
            taps[:, column:column + 128] = part.astype(BF16)


def tap_of(w_ref, tap):
    value = w_ref[tap].astype(F32)
    return jnp.concatenate([value, value], axis=1)


def widen(w_ref, wide, backward):
    low = lax.broadcasted_iota(jnp.int32, (1, 128), 1) < 64
    for tz in range(3):
        for q in range(9):
            tap = tz * 9 + q
            value = tap_of(w_ref, 26 - tap if backward else tap)
            a, b = (q, tz) if backward else (tz, q)
            lanes = pl.ds(b * 128, 128)
            wide[pl.ds(a * 128, 64), lanes] = jnp.where(low, value, 0.0).astype(BF16)
            wide[pl.ds(a * 128 + 64, 64), lanes] = jnp.where(low, 0.0, value).astype(BF16)


def convolve(taps, wide, backward=False):
    contract = (((1,), (0 if backward else 1,)), ((), ()))
    wide = lax.dot_general(taps[...], wide[...], contract, preferred_element_type=F32)
    return wide[0:512, 0:128] + wide[64:576, 128:256] + wide[128:640, 256:384]


def spread(wide_g, value):
    for tz in range(3):
        wide_g[tz * 64:tz * 64 + 512, tz * 128:tz * 128 + 128] = value


def clear_spread(wide_g):
    wide_g[...] = jnp.zeros((640, 384), BF16)


def outer(wide_g, taps):
    return lax.dot_general(
        wide_g[...], taps[...], (((0,), (0,)), ((), ())), preferred_element_type=F32
    )


def first_kernel(count_ref, par_ref, x_ref, g_ref, hx_ref, hg_ref, w_ref, v_ref,
                 h_out, fa_out, fb_out, m_out, cube, taps, taps_g, wide_g, scratch, wide_w, wide_v):
    pair = pl.program_id(0)

    @pl.when(pair == 0)
    def _():
        widen(w_ref, wide_w, False)
        widen(v_ref, wide_v, True)

    build_cube(cube, x_ref[0].astype(F32), hx_ref, par_ref, pair)
    stack_taps(cube, taps)
    first = convolve(taps, wide_w)
    hidden = jnp.where(live_lanes(count_ref, pair), jnp.maximum(first, 0.0), 0.0)
    hidden = hidden.astype(BF16).astype(F32)
    h_out[0] = hidden.astype(BF16)
    write_faces(hidden, scratch, (fa_out, fb_out), 0, 1)
    build_cube(cube, g_ref[0].astype(F32), hg_ref, par_ref, pair)
    stack_taps(cube, taps_g)
    back = convolve(taps_g, wide_v, True)
    hidden_grad = jnp.where(scratch[...] > 0, back, 0.0).astype(BF16)

    @pl.when(pair == 0)
    def _():
        clear_spread(wide_g)
        m_out[...] = jnp.zeros_like(m_out)

    spread(wide_g, hidden_grad)
    m_out[...] += outer(wide_g, taps)


def blocked(*shape):
    return pl.BlockSpec((1,) + shape, lambda p: (p,) + (0,) * len(shape))


def fixed(*shape):
    return pl.BlockSpec(shape, lambda p: (0,) * len(shape))


def halo_spec(field):
    return pl.BlockSpec((1, 2, 26, 64, 128), lambda p: (field, p, 0, 0, 0))


def first_part(counts, parity, xt, gt, halos, w, v):
    smem = pl.BlockSpec(memory_space=pltpu.SMEM)
    return pl.pallas_call(
        first_kernel,
        grid=(PAIRS,),
        in_specs=[smem, smem, blocked(512, 128), blocked(512, 128), halo_spec(0),
                  halo_spec(1), fixed(27, 64, 64), fixed(27, 64, 64)],
        out_specs=[blocked(512, 128), blocked(3, 64, 128), blocked(3, 64, 128),
                   fixed(384, 1152)],
        out_shape=[
            jax.ShapeDtypeStruct((PAIRS, 512, 128), BF16),
            jax.ShapeDtypeStruct((PAIRS, 3, 64, 128), BF16),
            jax.ShapeDtypeStruct((PAIRS, 3, 64, 128), BF16),
            jax.ShapeDtypeStruct((384, 1152), F32),
        ],
        scratch_shapes=[
            pltpu.VMEM((10, 10, 24, 128), F32),
            pltpu.VMEM((640, 1152), BF16),
            pltpu.VMEM((640, 1152), BF16),
            pltpu.VMEM((640, 384), BF16),
            pltpu.VMEM((512, 128), F32),
            pltpu.VMEM((384, 1152), BF16),
            pltpu.VMEM((1152, 384), BF16),
        ],
        compiler_params=pltpu.CompilerParams(vmem_limit_bytes=40 * 2**20),
    )(counts, parity, xt, gt, halos, halos, w, v)


def second_kernel(count_ref, par_ref, f_ref, h_ref, g_ref, hh_ref, w_ref, m1_ref,
                  o_out, p_out, cube, taps, wide_g, total, wide_w):
    pair = pl.program_id(0)

    @pl.when(pair == 0)
    def _():
        widen(w_ref, wide_w, False)

    build_cube(cube, h_ref[0].astype(F32), hh_ref, par_ref, pair)
    stack_taps(cube, taps)
    second = convolve(taps, wide_w)
    slot = 2 * pair + (lax.broadcasted_iota(jnp.int32, (128, 1), 0) >= 64).astype(jnp.int32)
    result = f_ref[0].astype(F32) + second.T
    o_out[0] = jnp.where(slot < own_count(count_ref), result, 0.0).astype(BF16)

    @pl.when(pair == 0)
    def _():
        clear_spread(wide_g)
        total[...] = jnp.zeros_like(total)

    spread(wide_g, g_ref[0])
    total[...] += outer(wide_g, taps)

    @pl.when(pair == PAIRS - 1)
    def _():
        low = lax.broadcasted_iota(jnp.int32, (1, 128), 1) < 64
        for q in range(9):
            for tz in range(3):
                even, odd = pl.ds(tz * 128, 64), pl.ds(tz * 128 + 64, 64)
                lanes = pl.ds(q * 128, 128)
                one = m1_ref[even, lanes] + pltpu.roll(m1_ref[odd, lanes], 64, 1)
                two = pltpu.roll(total[even, lanes], 64, 1) + total[odd, lanes]
                p_out[pl.ds((q * 3 + tz) * 64, 64), :] = jnp.where(low, one, two)
        p_out[1728:2048, :] = jnp.zeros((320, 128), F32)


def second_part(counts, parity, features, ht, gt, halos, v, m1):
    smem = pl.BlockSpec(memory_space=pltpu.SMEM)
    return pl.pallas_call(
        second_kernel,
        grid=(PAIRS,),
        in_specs=[smem, smem, blocked(128, 512), blocked(512, 128), blocked(512, 128),
                  halo_spec(0), fixed(27, 64, 64), fixed(384, 1152)],
        out_specs=[blocked(128, 512), fixed(2048, 128)],
        out_shape=[
            jax.ShapeDtypeStruct((PAIRS, 128, 512), BF16),
            jax.ShapeDtypeStruct((2048, 128), F32),
        ],
        scratch_shapes=[
            pltpu.VMEM((10, 10, 24, 128), F32),
            pltpu.VMEM((640, 1152), BF16),
            pltpu.VMEM((640, 384), BF16),
            pltpu.VMEM((384, 1152), F32),
            pltpu.VMEM((384, 1152), BF16),
        ],
        compiler_params=pltpu.CompilerParams(vmem_limit_bytes=40 * 2**20),
    )(counts, parity, features, ht, gt, halos, v, m1)


def reduce_kernel(p_ref, first_out, second_out, r1, a1, r2, r4, whole, send, recv):
    g, y, x, c = place()
    sibling = device(g, y, x, 1 - c)
    layer = [
        ((y + ky) % N_Y, (x + kx) % N_X, ky * N_X + kx)
        for ky in range(N_Y)
        for kx in range(N_X)
        if (ky, kx) != (0, 0)
    ]
    zs = [device((g + k) % N_Z, y, x, c) for k in range(1, N_Z)]
    greet([sibling] + [device(g, yy, xx, c) for yy, xx, _ in layer] + zs)
    used = [0]

    def copy(src, dst, target):
        number = used[0]
        used[0] += 1
        made = pltpu.make_async_remote_copy(
            src_ref=src, dst_ref=dst, send_sem=send.at[number], recv_sem=recv.at[number],
            device_id=target, device_id_type=MESH,
        )
        made.start()
        return made

    copy(p_ref.at[pl.ds((1 - c) * 1024, 1024)], r1, sibling).wait()
    a1[...] = (p_ref[pl.ds(c * 1024, 1024)] + r1[...]).astype(BF16)

    made = [
        copy(a1.at[pl.ds((yy * N_X + xx) * 64, 64)], r2.at[k], device(g, yy, xx, c))
        for yy, xx, k in layer
    ]
    for one in made:
        one.wait()
    at = y * N_X + x
    part = a1[pl.ds(at * 64, 64)].astype(F32)
    for k in range(1, 16):
        part = part + r2[k].astype(F32)
    r4[g] = part.astype(BF16)

    made = [copy(r4.at[g], r4.at[g], target) for target in zs]
    for one in made:
        one.wait()
    part = r4[0].astype(F32)
    for k in range(1, N_Z):
        part = part + r4[k].astype(F32)
    rows = pl.ds(c * 1024 + at * 64, 64)
    whole[rows] = part.astype(BF16)

    made = [
        copy(whole.at[rows], whole.at[rows], device(g, yy, xx, c)) for yy, xx, _ in layer
    ]
    for one in made:
        one.wait()
    half = pl.ds(c * 1024, 1024)
    copy(whole.at[half], whole.at[half], sibling).wait()
    for q in range(9):
        for tz in range(3):
            value = whole[pl.ds((q * 3 + tz) * 64, 64)].astype(F32)
            first_out[tz * 9 + q] = value[:, 0:64]
            second_out[tz * 9 + q] = pltpu.roll(value, 64, 1)[:, 0:64]


def reduce_all(p):
    return pl.pallas_call(
        reduce_kernel,
        in_specs=[pl.BlockSpec(memory_space=pltpu.VMEM)],
        out_specs=[pl.BlockSpec(memory_space=pltpu.VMEM)] * 2,
        out_shape=[jax.ShapeDtypeStruct((27, 64, 64), F32)] * 2,
        scratch_shapes=[
            pltpu.VMEM((1024, 128), F32),
            pltpu.VMEM((1024, 128), BF16),
            pltpu.VMEM((16, 64, 128), BF16),
            pltpu.VMEM((N_Z, 64, 128), BF16),
            pltpu.VMEM((2048, 128), BF16),
            pltpu.SemaphoreType.DMA((40,)),
            pltpu.SemaphoreType.DMA((40,)),
        ],
        compiler_params=pltpu.CompilerParams(
            collective_id=2, has_side_effects=True, vmem_limit_bytes=16 * 2**20
        ),
    )(p)


def halo_places(neighbours):
    halves = jnp.asarray(np.array([face_of(d)[0] for d in DIRECTIONS], np.int32))[None, :]
    dev = neighbours // 6 % 32
    y, x, c = dev // 8, dev // 2 % 4, dev % 2
    first = jnp.where(halves == 0, x, y)
    second = jnp.where(halves == 0, y, x)
    pos = ((c * 4 + second) * 4 + first) * 3 + neighbours % 6 // 2
    return jnp.where(neighbours >= 0, pos, 96).astype(jnp.int32), neighbours % 2


def per_device(features, cotangent, first_weight, second_weight, counts, neighbours):
    pos, parity = halo_places(neighbours)
    w1, w2 = first_weight.transpose(1, 0, 2), second_weight.transpose(1, 0, 2)
    feats = features.reshape(PAIRS, 128, 512)
    xt, gt, fa, fb = pack(counts, feats, cotangent.reshape(PAIRS, 128, 512))
    halos = gather(2, 0, pos, fa, fb)
    ht, ha, hb, m1 = first_part(counts, parity, xt, gt, halos, w1, w2)
    halos_h = gather(1, 1, pos, ha, hb)
    out, p = second_part(counts, parity, feats, ht, gt, halos_h, w2, m1)
    first_grad, second_grad = reduce_all(p)
    return (
        out.reshape(6, 64, 512),
        first_grad.transpose(1, 0, 2),
        second_grad.transpose(1, 0, 2),
    )


def solution(mesh):
    placed = (
        P(("group", "dev"), None, None),
        P(("group", "dev"), None, None),
        P(),
        P(),
        P(),
        P(("group", "dev"), None),
    )
    return jax.shard_map(
        per_device,
        mesh=mesh,
        in_specs=placed,
        out_specs=(P(("group", "dev"), None, None), P(), P()),
        check_vma=False,
    )
```

```python
import functools

import jax
import jax.numpy as jnp
import numpy as np
from jax import lax
from jax.experimental import pallas as pl
from jax.experimental.pallas import tpu as pltpu
from jax.sharding import PartitionSpec as P

MESH = pl.DeviceIdType.MESH
F32 = jnp.float32
BF16 = jnp.bfloat16
N_Z, N_Y, N_X = 8, 4, 4
PAIRS = 3
DIRECTIONS = [
    (dz, dy, dx)
    for dz in (-1, 0, 1)
    for dy in (-1, 0, 1)
    for dx in (-1, 0, 1)
    if (dz, dy, dx) != (0, 0, 0)
]


def face_of(direction):
    dz, dy, dx = direction
    if dz != 0:
        return (0 if dz == 1 else 1), 2
    if dx != 0:
        return (0 if dx == 1 else 1), 0
    return (0 if dy == 1 else 1), 1


def place():
    d = lax.axis_index("dev")
    return lax.axis_index("group"), d // 8, (d // 2) % 4, d % 2


def device(g, y, x, c):
    return (g, (y * 4 + x) * 2 + c)


class Gather:
    def __init__(self, field, bufs, zsrc, send, recv, started):
        self.field, self.bufs, self.zsrc = field, bufs, zsrc
        self.send, self.recv, self.started = send, recv, started
        self.g, self.y, self.x, self.c = place()
        self.mine = ((self.x, self.y), (self.y, self.x))
        self.axes = (("x", "y"), ("y", "x"))
        self.made = [dict(), dict()]

    def moved(self, axis, step):
        if axis == "x":
            return device(self.g, self.y, (self.x + step + N_X) % N_X, self.c)
        return device(self.g, (self.y + step + N_Y) % N_Y, self.x, self.c)

    def at(self, half, first):
        return ((self.c * 4 + self.mine[half][1]) * 4 + first) * 3

    def own(self, half):
        return self.at(half, self.mine[half][0])

    def row(self, half, step):
        return pl.ds((self.c * 4 + (self.mine[half][1] + step + 4) % 4) * 12, 12)

    def copy(self, half, number, src, dst, target):
        one = pltpu.make_async_remote_copy(
            src_ref=src,
            dst_ref=dst,
            send_sem=self.send.at[self.field, half, number],
            recv_sem=self.recv.at[self.field, half, number],
            device_id=target,
            device_id_type=MESH,
        )
        one.start()
        self.started.append(one)
        self.made[half][number] = one

    def same(self, half, number, index, target):
        part = self.bufs[half].at[index]
        self.copy(half, number, part, part, target)

    def came(self, half, *numbers):
        for number in numbers:
            self.made[half][number].wait_recv()

    def sibling(self):
        return device(self.g, self.y, self.x, 1 - self.c)

    def write(self, pair, value, scratch):
        scratch[...] = value
        cube = value.reshape(8, 8, 8, 128)
        for half, edge in ((0, 0), (1, 7)):
            at = self.own(half) + pair
            out = self.bufs[half]
            out[at, 0] = scratch[pl.ds(edge, 64, stride=8), :].astype(BF16)
            out[at, 1] = cube[:, edge].reshape(64, 128).astype(BF16)
            self.zsrc[half, pair, 0] = value[edge * 64:edge * 64 + 64].astype(BF16)

    def clear(self):
        for half in range(2):
            self.bufs[half][96:97] = jnp.zeros((1, 3, 64, 128), BF16)

    def layers(self):
        for half, step in ((0, N_Z - 1), (1, 1)):
            target = device((self.g + step) % N_Z, self.y, self.x, self.c)
            dst = self.bufs[half].at[pl.ds(self.own(half), 3), pl.ds(2, 1)]
            self.copy(half, 0, self.zsrc.at[half], dst, target)

    def step0(self):
        for half in range(2):
            self.came(half, 0)
            for number, step in ((1, 1), (2, -1)):
                block = pl.ds(self.own(half), 3)
                self.same(half, number, block, self.moved(self.axes[half][0], step))

    def step1(self):
        for number, step, rows in ((3, 1, pl.ds(0, 32)), (4, -1, pl.ds(32, 32))):
            for half in range(2):
                self.came(half, number - 2)
                block = pl.ds(self.at(half, (self.mine[half][0] - step + 4) % 4), 3)
                index = (block, slice(None), rows)
                self.same(half, number, index, self.moved(self.axes[half][0], step))

    def step2(self):
        for half in range(2):
            self.came(half, 3, 4)
            for number, step in ((5, 1), (6, -1)):
                target = self.moved(self.axes[half][1], step)
                self.same(half, number, self.row(half, 0), target)
            self.same(half, 9, self.row(half, 0), self.sibling())

    def step3(self):
        for number, step, rows in ((7, 1, pl.ds(0, 32)), (8, -1, pl.ds(32, 32))):
            for half in range(2):
                self.came(half, number - 2)
                index = (self.row(half, -step), slice(None), rows)
                self.same(half, number, index, self.moved(self.axes[half][1], step))
                self.same(half, number + 3, self.row(half, -step), self.sibling())

    def step4(self):
        for number, rows in ((7, pl.ds(0, 32)), (8, pl.ds(32, 32))):
            for half in range(2):
                self.came(half, number)
                index = (self.row(half, 2), slice(None), rows)
                self.same(half, number + 5, index, self.sibling())

    def step5(self):
        for half in range(2):
            self.came(half, 9, 10, 11, 12, 13)


def build_cube(cube, own, bufs, pos_ref, par_ref, pair):
    low = lax.broadcasted_iota(jnp.int32, (1, 128), 1) < 64
    cube[1:9, 1:9, 8:16, :] = own.reshape(8, 8, 8, 128)
    for k, (dz, dy, dx) in enumerate(DIRECTIONS):
        half, face = face_of((dz, dy, dx))
        if dz != 0 and dy != 0:
            start, count = (0, 16) if dy == 1 else (48, 16)
        else:
            start, count = 0, 64
        picked = []
        for s in range(2):
            at = pos_ref[2 * pair + s, k]
            value = bufs[half][at, face, start:start + count].astype(F32)
            turned = pltpu.roll(value, 64, 1)
            picked.append(jnp.where(par_ref[2 * pair + s, k] == s, value, turned))
        piece = jnp.where(low, picked[0], picked[1])
        if count == 16:
            piece = piece[0:8] if dy == 1 else piece[8:16]
        zz = {-1: 0, 1: 9}.get(dz)
        yy = {-1: 0, 1: 9}.get(dy)
        if dx == 0:
            if dz == 0:
                cube[1:9, yy, 8:16, :] = piece.reshape(8, 8, 128)
            elif dy == 0:
                cube[zz, 1:9, 8:16, :] = piece.reshape(8, 8, 128)
            else:
                cube[zz, yy, 8:16, :] = piece
            continue
        sub = 7 if dx == -1 else 16
        edge_x = 7 if dx == -1 else 0
        edge_y = 7 if dy == -1 else 0
        if dz == 0 and dy == 0:
            rows = [(z + 1, q + 1, z * 8 + q) for z in range(8) for q in range(8)]
        elif dz == 0:
            rows = [(z + 1, yy, z * 8 + edge_y) for z in range(8)]
        elif dy == 0:
            rows = [(zz, q + 1, q * 8 + edge_x) for q in range(8)]
        else:
            rows = [(zz, yy, edge_x)]
        for a, b, r in rows:
            cube[a, b, sub:sub + 1, :] = piece[r:r + 1]


def stack_taps(cube, taps, pair):
    for ty in range(3):
        for tx in range(3):
            part = cube[:, ty:ty + 8, 7 + tx:15 + tx, :].reshape(640, 128)
            column = (ty * 3 + tx) * 128
            taps[pair, :, column:column + 128] = part.astype(BF16)


def tap_of(w_ref, tap):
    value = w_ref[tap].astype(F32)
    return jnp.concatenate([value, value], axis=1)


def widen(w_ref, wide, backward):
    low = lax.broadcasted_iota(jnp.int32, (1, 128), 1) < 64
    for tz in range(3):
        for q in range(9):
            tap = tz * 9 + q
            value = tap_of(w_ref, 26 - tap if backward else tap)
            a, b = (q, tz) if backward else (tz, q)
            lanes = pl.ds(b * 128, 128)
            wide[pl.ds(a * 128, 64), lanes] = jnp.where(low, value, 0.0).astype(BF16)
            wide[pl.ds(a * 128 + 64, 64), lanes] = jnp.where(low, 0.0, value).astype(BF16)


def convolve(taps, wide, backward=False):
    contract = (((1,), (0 if backward else 1,)), ((), ()))
    wide = lax.dot_general(taps, wide[...], contract, preferred_element_type=F32)
    return wide[0:512, 0:128] + wide[64:576, 128:256] + wide[128:640, 256:384]


def spread(wide_g, pair, value):
    for tz in range(3):
        wide_g[pair, tz * 64:tz * 64 + 512, tz * 128:tz * 128 + 128] = value


def outer(wide_g, taps):
    return lax.dot_general(
        wide_g[...].reshape(PAIRS * 640, 384),
        taps[...].reshape(PAIRS * 640, 1152),
        (((0,), (0,)), ((), ())),
        preferred_element_type=F32,
    )


def block_kernel(count_ref, pos_ref, par_ref, f_ref, c_ref, w_ref, v_ref,
                 o_out, first_out, second_out,
                 xa, xb, ga, gb, ha, hb, zx, zg, zh, xs, gs, hs, scratch, cube, taps,
                 taps_g, wide_g, wide_w, wide_b, wide_v, product, p_sum,
                 r1, a1, r2, r4, whole, send, recv, send_sum, recv_sum):
    g, y, x, c = place()
    sibling = device(g, y, x, 1 - c)
    layer = [
        ((y + ky) % N_Y, (x + kx) % N_X, ky * N_X + kx)
        for ky in range(N_Y)
        for kx in range(N_X)
        if (ky, kx) != (0, 0)
    ]
    zs = [device((g + k) % N_Z, y, x, c) for k in range(1, N_Z)]
    partners = [sibling] + [device(g, yy, xx, c) for yy, xx, _ in layer] + zs
    barrier = pltpu.get_barrier_semaphore()
    for partner in partners:
        pl.semaphore_signal(barrier, inc=1, device_id=partner, device_id_type=MESH)

    count = count_ref[g, lax.axis_index("dev")]
    low = lax.broadcasted_iota(jnp.int32, (1, 128), 1) < 64
    started = []
    gx = Gather(0, (xa, xb), zx, send, recv, started)
    gg = Gather(1, (ga, gb), zg, send, recv, started)
    gh = Gather(2, (ha, hb), zh, send, recv, started)

    def live(pair):
        return jnp.where(low, 2 * pair, 2 * pair + 1) < count

    def over_pairs(body):
        def step(pair, carry):
            body(pair)
            return carry

        lax.fori_loop(0, PAIRS, step, 0)

    def pack_x(pair):
        value = f_ref[pair].astype(F32).T
        xs[pair] = value.astype(BF16)
        gx.write(pair, value, scratch)

    def pack_g(pair):
        value = jnp.where(live(pair), c_ref[pair].astype(F32).T, 0.0)
        gs[pair] = value.astype(BF16)
        gg.write(pair, value, scratch)

    def forward(pair):
        build_cube(cube, xs[pair].astype(F32), gx.bufs, pos_ref, par_ref, pair)
        stack_taps(cube, taps, pair)
        first = convolve(taps[pair], wide_w)
        hidden = jnp.where(live(pair), jnp.maximum(first, 0.0), 0.0)
        hidden = hidden.astype(BF16).astype(F32)
        hs[pair] = hidden.astype(BF16)
        gh.write(pair, hidden, scratch)

    def backward(pair):
        build_cube(cube, gs[pair].astype(F32), gg.bufs, pos_ref, par_ref, pair)
        stack_taps(cube, taps_g, 0)
        back = convolve(taps_g[0], wide_b, True)
        grad = jnp.where(hs[pair].astype(F32) > 0, back, 0.0)
        spread(wide_g, pair, grad.astype(BF16))

    def stack_h(pair):
        build_cube(cube, hs[pair].astype(F32), gh.bufs, pos_ref, par_ref, pair)
        stack_taps(cube, taps, pair)
        spread(wide_g, pair, gs[pair])

    def finish(pair):
        second = convolve(taps[pair], wide_v)
        lane = lax.broadcasted_iota(jnp.int32, (128, 1), 0)
        slot = jnp.where(lane < 64, 2 * pair, 2 * pair + 1)
        result = f_ref[pair].astype(F32) + second.T
        o_out[pair] = jnp.where(slot < count, result, 0.0).astype(BF16)

    over_pairs(pack_x)
    pl.semaphore_wait(barrier, len(partners))
    gx.layers()
    over_pairs(pack_g)
    gg.layers()
    gx.step0()
    for one in (gx, gg, gh):
        one.clear()
    widen(w_ref, wide_w, False)
    gx.step1()
    widen(v_ref, wide_b, True)
    gx.step2()
    widen(v_ref, wide_v, False)
    wide_g[...] = jnp.zeros((PAIRS, 640, 384), BF16)
    gx.step3()
    gg.step0()
    gx.step4()
    gg.step1()
    gx.step5()
    over_pairs(forward)
    gh.layers()
    gg.step2()
    gh.step0()
    gh.step1()
    gh.step2()
    gg.step3()
    gg.step4()
    gg.step5()
    over_pairs(backward)
    gh.step3()
    product[...] = outer(wide_g, taps)
    for q in range(9):
        for tz in range(3):
            even, odd = pl.ds(tz * 128, 64), pl.ds(tz * 128 + 64, 64)
            lanes = pl.ds(q * 128, 128)
            one = product[even, lanes] + pltpu.roll(product[odd, lanes], 64, 1)
            p_sum[pl.ds((q * 3 + tz) * 64, 64), :] = one
    p_sum[1728:2048, :] = jnp.zeros((320, 128), F32)
    gh.step4()
    gh.step5()
    over_pairs(stack_h)
    product[...] = outer(wide_g, taps)
    for q in range(9):
        for tz in range(3):
            even, odd = pl.ds(tz * 128, 64), pl.ds(tz * 128 + 64, 64)
            lanes = pl.ds(q * 128, 128)
            rows = pl.ds((q * 3 + tz) * 64, 64)
            two = pltpu.roll(product[even, lanes], 64, 1) + product[odd, lanes]
            p_sum[rows, :] = jnp.where(low, p_sum[rows, :], two)

    used = [0]

    def copy(src, dst, target):
        number = used[0]
        used[0] += 1
        one = pltpu.make_async_remote_copy(
            src_ref=src, dst_ref=dst, send_sem=send_sum.at[number],
            recv_sem=recv_sum.at[number], device_id=target, device_id_type=MESH,
        )
        one.start()
        return one

    one = copy(p_sum.at[pl.ds((1 - c) * 1024, 1024)], r1, sibling)
    finish(0)
    one.wait()
    a1[...] = (p_sum[pl.ds(c * 1024, 1024)] + r1[...]).astype(BF16)

    made = [
        copy(a1.at[pl.ds((yy * N_X + xx) * 64, 64)], r2.at[k], device(g, yy, xx, c))
        for yy, xx, k in layer
    ]
    finish(1)
    for one in made:
        one.wait()
    at = y * N_X + x
    part = a1[pl.ds(at * 64, 64)].astype(F32)
    for k in range(1, 16):
        part = part + r2[k].astype(F32)
    r4[g] = part.astype(BF16)

    made = [copy(r4.at[g], r4.at[g], target) for target in zs]
    finish(2)
    for one in made:
        one.wait()
    part = r4[0].astype(F32)
    for k in range(1, N_Z):
        part = part + r4[k].astype(F32)
    rows = pl.ds(c * 1024 + at * 64, 64)
    whole[rows] = part.astype(BF16)

    made = [
        copy(whole.at[rows], whole.at[rows], device(g, yy, xx, c)) for yy, xx, _ in layer
    ]
    for one in made:
        one.wait()
    half = pl.ds(c * 1024, 1024)
    copy(whole.at[half], whole.at[half], sibling).wait()
    for q in range(9):
        for tz in range(3):
            value = whole[pl.ds((q * 3 + tz) * 64, 64)].astype(F32)
            first_out[tz * 9 + q] = value[:, 0:64]
            second_out[tz * 9 + q] = pltpu.roll(value, 64, 1)[:, 0:64]
    for one in started:
        one.wait_send()


def block(counts, pos, parity, features, cotangent, w, v):
    smem, vmem = pl.BlockSpec(memory_space=pltpu.SMEM), pl.BlockSpec(memory_space=pltpu.VMEM)
    return pl.pallas_call(
        block_kernel,
        in_specs=[smem] * 3 + [vmem] * 4,
        out_specs=[vmem] * 3,
        out_shape=[
            jax.ShapeDtypeStruct((PAIRS, 128, 512), BF16),
            jax.ShapeDtypeStruct((27, 64, 64), F32),
            jax.ShapeDtypeStruct((27, 64, 64), F32),
        ],
        scratch_shapes=[pltpu.VMEM((97, 3, 64, 128), BF16)] * 6
        + [pltpu.VMEM((2, PAIRS, 1, 64, 128), BF16)] * 3
        + [pltpu.VMEM((PAIRS, 512, 128), BF16)] * 3
        + [
            pltpu.VMEM((512, 128), F32),
            pltpu.VMEM((10, 10, 24, 128), F32),
            pltpu.VMEM((PAIRS, 640, 1152), BF16),
            pltpu.VMEM((1, 640, 1152), BF16),
            pltpu.VMEM((PAIRS, 640, 384), BF16),
            pltpu.VMEM((384, 1152), BF16),
            pltpu.VMEM((1152, 384), BF16),
            pltpu.VMEM((384, 1152), BF16),
            pltpu.VMEM((384, 1152), F32),
            pltpu.VMEM((2048, 128), F32),
            pltpu.VMEM((1024, 128), F32),
            pltpu.VMEM((1024, 128), BF16),
            pltpu.VMEM((16, 64, 128), BF16),
            pltpu.VMEM((N_Z, 64, 128), BF16),
            pltpu.VMEM((2048, 128), BF16),
            pltpu.SemaphoreType.DMA((3, 2, 14)),
            pltpu.SemaphoreType.DMA((3, 2, 14)),
            pltpu.SemaphoreType.DMA((40,)),
            pltpu.SemaphoreType.DMA((40,)),
        ],
        compiler_params=pltpu.CompilerParams(
            collective_id=0, has_side_effects=True, vmem_limit_bytes=62 * 2**20
        ),
    )(counts, pos, parity, features, cotangent, w, v)


def halo_places(neighbours):
    halves = jnp.asarray(np.array([face_of(d)[0] for d in DIRECTIONS], np.int32))[None, :]
    dev = neighbours // 6 % 32
    y, x, c = dev // 8, dev // 2 % 4, dev % 2
    first = jnp.where(halves == 0, x, y)
    second = jnp.where(halves == 0, y, x)
    pos = ((c * 4 + second) * 4 + first) * 3 + neighbours % 6 // 2
    return jnp.where(neighbours >= 0, pos, 96).astype(jnp.int32), neighbours % 2


def per_device(features, cotangent, first_weight, second_weight, counts, neighbours):
    pos, parity = halo_places(neighbours)
    out, first_grad, second_grad = block(
        counts,
        pos,
        parity,
        features.reshape(PAIRS, 128, 512),
        cotangent.reshape(PAIRS, 128, 512),
        first_weight.transpose(1, 0, 2),
        second_weight.transpose(1, 0, 2),
    )
    return (
        out.reshape(6, 64, 512),
        first_grad.transpose(1, 0, 2),
        second_grad.transpose(1, 0, 2),
    )


def solution(mesh):
    placed = (
        P(("group", "dev"), None, None),
        P(("group", "dev"), None, None),
        P(),
        P(),
        P(),
        P(("group", "dev"), None),
    )
    return jax.shard_map(
        per_device,
        mesh=mesh,
        in_specs=placed,
        out_specs=(P(("group", "dev"), None, None), P(), P()),
        check_vma=False,
    )
```

```python
import functools

import jax
import jax.numpy as jnp
import numpy as np
from jax import lax
from jax.experimental import pallas as pl
from jax.experimental.pallas import tpu as pltpu
from jax.sharding import PartitionSpec as P

MESH = pl.DeviceIdType.MESH
F32 = jnp.float32
BF16 = jnp.bfloat16
N_Z, N_Y, N_X = 8, 4, 4
PAIRS = 3
DIRECTIONS = [
    (dz, dy, dx)
    for dz in (-1, 0, 1)
    for dy in (-1, 0, 1)
    for dx in (-1, 0, 1)
    if (dz, dy, dx) != (0, 0, 0)
]


def face_of(direction):
    dz, dy, dx = direction
    if dz != 0:
        return (0 if dz == 1 else 1), 2
    if dx != 0:
        return (0 if dx == 1 else 1), 0
    return (0 if dy == 1 else 1), 1


def place():
    d = lax.axis_index("dev")
    return lax.axis_index("group"), d // 8, (d // 2) % 4, d % 2


def device(g, y, x, c):
    return (g, (y * 4 + x) * 2 + c)


class Gather:
    def __init__(self, field, cap, list_ref, rows, line, src, send, recv, started):
        self.field, self.cap, self.list_ref = field, cap, list_ref
        self.rows, self.line, self.src = rows, line, src
        self.send, self.recv, self.started = send, recv, started
        self.g, self.y, self.x, self.c = place()
        self.i = self.first(self.c)
        self.j = self.first(1 - self.c)
        self.made = dict()

    def first(self, half):
        return self.x * (1 - half) + self.y * half

    def moved(self, first, step):
        along_y = self.c if first else 1 - self.c
        y = (self.y + step * along_y + N_Y) % N_Y
        x = (self.x + step * (1 - along_y) + N_X) % N_X
        return device(self.g, y, x, self.c)

    def row(self, step):
        return pl.ds((self.j + step + 4) % 4 * 24, self.cap)

    def block(self, step):
        return pl.ds((self.i + step + 4) % 4 * 6, 6)

    def sibling(self):
        return device(self.g, self.y, self.x, 1 - self.c)

    def describe(self, number, came, src, dst, target):
        return pltpu.make_async_remote_copy(
            src_ref=src,
            dst_ref=dst,
            send_sem=self.send.at[self.field, number],
            recv_sem=self.recv.at[self.field, came],
            device_id=target,
            device_id_type=MESH,
        )

    def copy(self, number, came, src, dst, target):
        one = self.describe(number, came, src, dst, target)
        one.start()
        self.started.append(one)
        self.made[number] = one

    def same(self, number, part, target):
        self.copy(number, number, part, part, target)

    def came(self, *numbers):
        for number in numbers:
            self.made[number].wait_recv()

    def write(self, pair, value, scratch):
        scratch[...] = value
        cube = value.reshape(8, 8, 8, 128)
        for half, edge in ((0, 0), (1, 7)):
            self.src[half, pair, 0] = scratch[pl.ds(edge, 64, stride=8), :].astype(BF16)
            self.src[half, pair, 1] = cube[:, edge].reshape(64, 128).astype(BF16)
            self.src[half, pair, 2] = value[edge * 64:edge * 64 + 64].astype(BF16)

    def clear(self):
        for half in range(2):
            self.rows[half, 96:97] = jnp.zeros((1, 3, 64, 128), BF16)

    def begin(self):
        sides, plane, c = pl.ds(0, 2), pl.ds(2, 1), self.c
        for half, step in ((0, N_Z - 1), (1, 1)):
            target = device((self.g + step) % N_Z, self.y, self.x, half)
            dst = self.line.at[pl.ds(self.first(half) * 6 + c * 3, 3), plane]
            self.copy(1 + half, 1 + c, self.src.at[half, :, plane], dst, target)
        dst = self.line.at[pl.ds(self.first(1 - c) * 6 + c * 3, 3), sides]
        self.copy(0, 0, self.src.at[1 - c, :, sides], dst, self.sibling())
        self.line[pl.ds(self.i * 6 + c * 3, 3), 0:2] = self.src[c, :, 0:2]

    def step0(self):
        self.came(0)
        part = self.line.at[pl.ds(0, 3), pl.ds(2, 1)]
        for core in range(2):
            self.describe(1, 1 + core, part, part, self.sibling()).wait_recv()
        for number, step in ((3, 1), (4, -1)):
            self.same(number, self.line.at[self.block(0)], self.moved(True, step))

    def step1(self):
        for number, step, rows in ((5, 1, pl.ds(0, 32)), (6, -1, pl.ds(32, 32))):
            self.came(number - 2)
            part = self.line.at[self.block(-step), :, rows]
            self.same(number, part, self.moved(True, step))

    def step2(self):
        self.came(5, 6)

        def one(k, carry):
            at = self.j * 24 + k
            self.rows[self.c, at, 0:2] = self.line[self.list_ref[0, k], 0:2]
            self.rows[self.c, at, 2:3] = self.line[self.list_ref[1, k], 2:3]
            return carry

        lax.fori_loop(0, self.cap, one, 0)
        part = self.rows.at[self.c, self.row(0)]
        for number, step in ((7, 1), (8, -1)):
            self.same(number, part, self.moved(False, step))
        self.same(11, part, self.sibling())

    def step3(self):
        for number, step, rows in ((9, 1, pl.ds(0, 32)), (10, -1, pl.ds(32, 32))):
            self.came(number - 2)
            part = self.rows.at[self.c, self.row(-step), :, rows]
            self.same(number, part, self.moved(False, step))
            self.same(number + 3, self.rows.at[self.c, self.row(-step)], self.sibling())

    def step4(self):
        for number, rows in ((9, pl.ds(0, 32)), (10, pl.ds(32, 32))):
            self.came(number)
            part = self.rows.at[self.c, self.row(2), :, rows]
            self.same(number + 5, part, self.sibling())

    def step5(self):
        self.came(11, 12, 13, 14, 15)


def build_cube(cube, own, rows_ref, pos_ref, par_ref, pair):
    low = lax.broadcasted_iota(jnp.int32, (1, 128), 1) < 64
    cube[1:9, 1:9, 8:16, :] = own.reshape(8, 8, 8, 128)
    for k, (dz, dy, dx) in enumerate(DIRECTIONS):
        half, face = face_of((dz, dy, dx))
        if dz != 0 and dy != 0:
            start, count = (0, 16) if dy == 1 else (48, 16)
        else:
            start, count = 0, 64
        picked = []
        for s in range(2):
            at = pos_ref[2 * pair + s, k]
            value = rows_ref[half, at, face, start:start + count].astype(F32)
            turned = pltpu.roll(value, 64, 1)
            picked.append(jnp.where(par_ref[2 * pair + s, k] == s, value, turned))
        piece = jnp.where(low, picked[0], picked[1])
        if count == 16:
            piece = piece[0:8] if dy == 1 else piece[8:16]
        zz = {-1: 0, 1: 9}.get(dz)
        yy = {-1: 0, 1: 9}.get(dy)
        if dx == 0:
            if dz == 0:
                cube[1:9, yy, 8:16, :] = piece.reshape(8, 8, 128)
            elif dy == 0:
                cube[zz, 1:9, 8:16, :] = piece.reshape(8, 8, 128)
            else:
                cube[zz, yy, 8:16, :] = piece
            continue
        sub = 7 if dx == -1 else 16
        edge_x = 7 if dx == -1 else 0
        edge_y = 7 if dy == -1 else 0
        if dz == 0 and dy == 0:
            rows = [(z + 1, q + 1, z * 8 + q) for z in range(8) for q in range(8)]
        elif dz == 0:
            rows = [(z + 1, yy, z * 8 + edge_y) for z in range(8)]
        elif dy == 0:
            rows = [(zz, q + 1, q * 8 + edge_x) for q in range(8)]
        else:
            rows = [(zz, yy, edge_x)]
        for a, b, r in rows:
            cube[a, b, sub:sub + 1, :] = piece[r:r + 1]


def stack_taps(cube, taps, pair):
    for ty in range(3):
        for tx in range(3):
            part = cube[:, ty:ty + 8, 7 + tx:15 + tx, :].reshape(640, 128)
            column = (ty * 3 + tx) * 128
            taps[pair, :, column:column + 128] = part.astype(BF16)


def tap_of(w_ref, tap):
    value = w_ref[tap].astype(F32)
    return jnp.concatenate([value, value], axis=1)


def widen(w_ref, wide, backward):
    low = lax.broadcasted_iota(jnp.int32, (1, 128), 1) < 64
    for tz in range(3):
        for q in range(9):
            tap = tz * 9 + q
            value = tap_of(w_ref, 26 - tap if backward else tap)
            a, b = (q, tz) if backward else (tz, q)
            lanes = pl.ds(b * 128, 128)
            wide[pl.ds(a * 128, 64), lanes] = jnp.where(low, value, 0.0).astype(BF16)
            wide[pl.ds(a * 128 + 64, 64), lanes] = jnp.where(low, 0.0, value).astype(BF16)


def convolve(taps, wide, backward=False):
    contract = (((1,), (0 if backward else 1,)), ((), ()))
    wide = lax.dot_general(taps, wide[...], contract, preferred_element_type=F32)
    return wide[0:512, 0:128] + wide[64:576, 128:256] + wide[128:640, 256:384]


def spread(wide_g, pair, value):
    for tz in range(3):
        wide_g[pair, tz * 64:tz * 64 + 512, tz * 128:tz * 128 + 128] = value


def outer(wide_g, taps):
    return lax.dot_general(
        wide_g[...].reshape(PAIRS * 640, 384),
        taps[...].reshape(PAIRS * 640, 1152),
        (((0,), (0,)), ((), ())),
        preferred_element_type=F32,
    )


def block_kernel(cap, count_ref, list_ref, pos_ref, par_ref, f_ref, c_ref, w_ref, v_ref,
                 o_out, grads_out,
                 rows_x, rows_g, rows_h, line_x, line_g, line_h, src_x, src_g, src_h, xs, gs, hs, scratch, cube, taps,
                 taps_g, wide_g, wide_w, wide_b, wide_v, product, p_sum,
                 r1, a1, r2, r4, whole, send, recv, send_sum, recv_sum):
    g, y, x, c = place()
    sibling = device(g, y, x, 1 - c)
    layer = [
        ((y + ky) % N_Y, (x + kx) % N_X, ky * N_X + kx)
        for ky in range(N_Y)
        for kx in range(N_X)
        if (ky, kx) != (0, 0)
    ]
    zs = [device((g + k) % N_Z, y, x, c) for k in range(1, N_Z)]
    partners = [sibling] + [device(g, yy, xx, c) for yy, xx, _ in layer] + zs
    partners += [device((g + k) % N_Z, y, x, 1 - c) for k in (1, N_Z - 1)]
    barrier = pltpu.get_barrier_semaphore()
    for partner in partners:
        pl.semaphore_signal(barrier, inc=1, device_id=partner, device_id_type=MESH)

    count = count_ref[g, lax.axis_index("dev")]
    low = lax.broadcasted_iota(jnp.int32, (1, 128), 1) < 64
    started = []
    gx = Gather(0, cap, list_ref, rows_x, line_x, src_x, send, recv, started)
    gg = Gather(1, cap, list_ref, rows_g, line_g, src_g, send, recv, started)
    gh = Gather(2, cap, list_ref, rows_h, line_h, src_h, send, recv, started)

    def live(pair):
        return jnp.where(low, 2 * pair, 2 * pair + 1) < count

    def over_pairs(body):
        def step(pair, carry):
            body(pair)
            return carry

        lax.fori_loop(0, PAIRS, step, 0)

    def pack_x(pair):
        value = f_ref[pair].astype(F32).T
        xs[pair] = value.astype(BF16)
        gx.write(pair, value, scratch)

    def pack_g(pair):
        value = jnp.where(live(pair), c_ref[pair].astype(F32).T, 0.0)
        gs[pair] = value.astype(BF16)
        gg.write(pair, value, scratch)

    def forward(pair):
        build_cube(cube, xs[pair].astype(F32), rows_x, pos_ref, par_ref, pair)
        stack_taps(cube, taps, pair)
        first = convolve(taps[pair], wide_w)
        hidden = jnp.where(live(pair), jnp.maximum(first, 0.0), 0.0)
        hidden = hidden.astype(BF16).astype(F32)
        hs[pair] = hidden.astype(BF16)
        gh.write(pair, hidden, scratch)

    def backward(pair):
        build_cube(cube, gs[pair].astype(F32), rows_g, pos_ref, par_ref, pair)
        stack_taps(cube, taps_g, 0)
        back = convolve(taps_g[0], wide_b, True)
        grad = jnp.where(hs[pair].astype(F32) > 0, back, 0.0)
        spread(wide_g, pair, grad.astype(BF16))

    def stack_h(pair):
        build_cube(cube, hs[pair].astype(F32), rows_h, pos_ref, par_ref, pair)
        stack_taps(cube, taps, pair)
        spread(wide_g, pair, gs[pair])

    def finish(pair):
        second = convolve(taps[pair], wide_v)
        lane = lax.broadcasted_iota(jnp.int32, (128, 1), 0)
        slot = jnp.where(lane < 64, 2 * pair, 2 * pair + 1)
        result = f_ref[pair].astype(F32) + second.T
        o_out[pair] = jnp.where(slot < count, result, 0.0).astype(BF16)

    over_pairs(pack_x)
    pl.semaphore_wait(barrier, len(partners))
    gx.begin()
    over_pairs(pack_g)
    gg.begin()
    gx.step0()
    for one in (gx, gg, gh):
        one.clear()
    widen(w_ref, wide_w, False)
    gx.step1()
    gg.step0()
    gx.step2()
    gg.step1()
    widen(v_ref, wide_b, True)
    widen(v_ref, wide_v, False)
    wide_g[...] = jnp.zeros((PAIRS, 640, 384), BF16)
    gx.step3()
    gx.step4()
    gg.step2()
    gx.step5()
    over_pairs(forward)
    gh.begin()
    gh.step0()
    gh.step1()
    gg.step3()
    gh.step2()
    gg.step4()
    gg.step5()
    over_pairs(backward)
    gh.step3()
    product[...] = outer(wide_g, taps)
    for q in range(9):
        for tz in range(3):
            even, odd = pl.ds(tz * 128, 64), pl.ds(tz * 128 + 64, 64)
            lanes = pl.ds(q * 128, 128)
            one = product[even, lanes] + pltpu.roll(product[odd, lanes], 64, 1)
            p_sum[pl.ds((q * 3 + tz) * 64, 64), :] = one
    p_sum[1728:2048, :] = jnp.zeros((320, 128), F32)
    gh.step4()
    gh.step5()
    over_pairs(stack_h)
    product[...] = outer(wide_g, taps)
    for q in range(9):
        for tz in range(3):
            even, odd = pl.ds(tz * 128, 64), pl.ds(tz * 128 + 64, 64)
            lanes = pl.ds(q * 128, 128)
            rows = pl.ds((q * 3 + tz) * 64, 64)
            two = pltpu.roll(product[even, lanes], 64, 1) + product[odd, lanes]
            p_sum[rows, :] = jnp.where(low, p_sum[rows, :], two)

    used = [0]

    def copy(src, dst, target):
        number = used[0]
        used[0] += 1
        one = pltpu.make_async_remote_copy(
            src_ref=src, dst_ref=dst, send_sem=send_sum.at[number],
            recv_sem=recv_sum.at[number], device_id=target, device_id_type=MESH,
        )
        one.start()
        return one

    one = copy(p_sum.at[pl.ds((1 - c) * 1024, 1024)], r1, sibling)
    finish(0)
    one.wait()
    a1[...] = (p_sum[pl.ds(c * 1024, 1024)] + r1[...]).astype(BF16)

    made = [
        copy(a1.at[pl.ds((yy * N_X + xx) * 64, 64)], r2.at[k], device(g, yy, xx, c))
        for yy, xx, k in layer
    ]
    finish(1)
    for one in made:
        one.wait()
    at = y * N_X + x
    part = a1[pl.ds(at * 64, 64)].astype(F32)
    for k in range(1, 16):
        part = part + r2[k].astype(F32)
    r4[g] = part.astype(BF16)

    made = [copy(r4.at[g], r4.at[g], target) for target in zs]
    finish(2)
    for one in made:
        one.wait()
    part = r4[0].astype(F32)
    for k in range(1, N_Z):
        part = part + r4[k].astype(F32)
    rows = pl.ds(c * 1024 + at * 64, 64)
    whole[rows] = part.astype(BF16)

    made = [
        copy(whole.at[rows], whole.at[rows], device(g, yy, xx, c)) for yy, xx, _ in layer
    ]
    for one in made:
        one.wait()
    half = pl.ds(c * 1024, 1024)
    copy(whole.at[half], whole.at[half], sibling).wait()
    for q in range(9):
        for tz in range(3):
            grads_out[tz * 9 + q] = whole[pl.ds((q * 3 + tz) * 64, 64)]
    for one in started:
        one.wait_send()


def block(cap, collective_id, counts, lists, pos, parity, features, cotangent, w, v):
    smem, vmem = pl.BlockSpec(memory_space=pltpu.SMEM), pl.BlockSpec(memory_space=pltpu.VMEM)
    return pl.pallas_call(
        functools.partial(block_kernel, cap),
        in_specs=[smem] * 4 + [vmem] * 4,
        out_specs=[vmem] * 2,
        out_shape=[
            jax.ShapeDtypeStruct((PAIRS, 128, 512), BF16),
            jax.ShapeDtypeStruct((27, 64, 128), BF16),
        ],
        scratch_shapes=[pltpu.VMEM((2, 97, 3, 64, 128), BF16)] * 3
        + [pltpu.VMEM((24, 3, 64, 128), BF16)] * 3
        + [pltpu.VMEM((2, PAIRS, 3, 64, 128), BF16)] * 3
        + [pltpu.VMEM((PAIRS, 512, 128), BF16)] * 3
        + [
            pltpu.VMEM((512, 128), F32),
            pltpu.VMEM((10, 10, 24, 128), F32),
            pltpu.VMEM((PAIRS, 640, 1152), BF16),
            pltpu.VMEM((1, 640, 1152), BF16),
            pltpu.VMEM((PAIRS, 640, 384), BF16),
            pltpu.VMEM((384, 1152), BF16),
            pltpu.VMEM((1152, 384), BF16),
            pltpu.VMEM((384, 1152), BF16),
            pltpu.VMEM((384, 1152), F32),
            pltpu.VMEM((2048, 128), F32),
            pltpu.VMEM((1024, 128), F32),
            pltpu.VMEM((1024, 128), BF16),
            pltpu.VMEM((16, 64, 128), BF16),
            pltpu.VMEM((N_Z, 64, 128), BF16),
            pltpu.VMEM((2048, 128), BF16),
            pltpu.SemaphoreType.DMA((3, 16)),
            pltpu.SemaphoreType.DMA((3, 16)),
            pltpu.SemaphoreType.DMA((40,)),
            pltpu.SemaphoreType.DMA((40,)),
        ],
        compiler_params=pltpu.CompilerParams(
            collective_id=collective_id, has_side_effects=True, vmem_limit_bytes=62 * 2**20
        ),
    )(counts, lists, pos, parity, features, cotangent, w, v)


def tables(counts, neighbours):
    d = np.arange(32)
    row = np.stack([d // 8, d // 2 % 4]).astype(np.int32)
    order = np.stack([d // 2 % 4 * 2 + d % 2, d // 8 * 2 + d % 2]).astype(np.int32)
    before = (row[:, :, None] == row[:, None, :]) & (order[:, None, :] < order[:, :, None])
    pairs = (counts + 1) // 2
    base = jnp.sum(jnp.where(before[:, None], pairs[None, :, None, :], 0), axis=3)
    needed = jnp.max(base + pairs[None])

    halves = np.array([face_of(k)[0] for k in DIRECTIONS], np.int32)[None, :]
    dev = neighbours // 6 % 32
    hit = (neighbours // 6)[:, :, None] == np.arange(256, dtype=np.int32)
    bases = jnp.where(halves[:, :, None] == 0, base[0].reshape(256), base[1].reshape(256))
    rank = jnp.sum(jnp.where(hit, bases, 0), axis=2) + neighbours % 6 // 2
    pos = jnp.where(halves == 0, dev // 8, dev // 2 % 4) * 24 + rank
    pos = jnp.where(neighbours >= 0, pos, 96).astype(jnp.int32)

    g, y, x, c = place()
    own_row = jnp.where(c == 0, y, x)
    rows, orders = jnp.where(c == 0, row[0], row[1]), jnp.where(c == 0, order[0], order[1])
    groups = jnp.stack([g, (g + jnp.where(c == 0, 1, N_Z - 1)) % N_Z])
    p = np.arange(3, dtype=np.int32)
    ranks = jnp.where(c == 0, base[0], base[1])[:, :, None] + p
    sent = (rows == own_row)[None, :, None] & (p < pairs[:, :, None])
    here = np.arange(N_Z, dtype=np.int32)[None, :] == groups[:, None]
    match = (
        here[:, None, :, None, None]
        & sent[None, None]
        & (ranks[None, None] == np.arange(24, dtype=np.int32)[None, :, None, None, None])
    )
    lists = jnp.sum(jnp.where(match, (orders[:, None] * 3 + p)[None, None, None], 0), axis=(2, 3, 4))
    return needed, lists.astype(jnp.int32), pos, neighbours % 2


def per_device(features, cotangent, first_weight, second_weight, counts, neighbours):
    needed, lists, pos, parity = tables(counts, neighbours)
    operands = (
        counts,
        lists,
        pos,
        parity,
        features.reshape(PAIRS, 128, 512),
        cotangent.reshape(PAIRS, 128, 512),
        first_weight.transpose(1, 0, 2),
        second_weight.transpose(1, 0, 2),
    )
    out, grads = lax.cond(
        needed <= 16,
        functools.partial(block, 16, 0),
        functools.partial(block, 24, 1),
        *operands,
    )
    return (
        out.reshape(6, 64, 512),
        grads[:, :, :64].astype(F32).transpose(1, 0, 2),
        grads[:, :, 64:].astype(F32).transpose(1, 0, 2),
    )


def solution(mesh):
    placed = (
        P(("group", "dev"), None, None),
        P(("group", "dev"), None, None),
        P(),
        P(),
        P(),
        P(("group", "dev"), None),
    )
    return jax.shard_map(
        per_device,
        mesh=mesh,
        in_specs=placed,
        out_specs=(P(("group", "dev"), None, None), P(), P()),
        check_vma=False,
    )
```

```python
import functools

import jax
import jax.numpy as jnp
import numpy as np
from jax import lax
from jax.experimental import pallas as pl
from jax.experimental.pallas import tpu as pltpu
from jax.sharding import PartitionSpec as P

MESH = pl.DeviceIdType.MESH
F32 = jnp.float32
BF16 = jnp.bfloat16
N_Z, N_Y, N_X = 8, 4, 4
PAIRS = 3
CAPS = (14, 16, 24)
DIRECTIONS = [
    (dz, dy, dx)
    for dz in (-1, 0, 1)
    for dy in (-1, 0, 1)
    for dx in (-1, 0, 1)
    if (dz, dy, dx) != (0, 0, 0)
]


def face_of(direction):
    dz, dy, dx = direction
    if dz != 0:
        return (0 if dz == 1 else 1), 2
    if dx != 0:
        return (0 if dx == 1 else 1), 0
    return (0 if dy == 1 else 1), 1


def place():
    d = lax.axis_index("dev")
    return lax.axis_index("group"), d // 8, (d // 2) % 4, d % 2


def device(g, y, x, c):
    return (g, (y * 4 + x) * 2 + c)


class Gather:
    def __init__(self, field, cap, list_ref, rows, line, src, send, recv, started):
        self.field, self.cap, self.list_ref = field, cap, list_ref
        self.rows, self.line, self.src = rows, line, src
        self.send, self.recv, self.started = send, recv, started
        self.g, self.y, self.x, self.c = place()
        self.i = self.first(self.c)
        self.j = self.first(1 - self.c)
        self.made = dict()

    def first(self, half):
        return self.x * (1 - half) + self.y * half

    def moved(self, first, step):
        along_y = self.c if first else 1 - self.c
        y = (self.y + step * along_y + N_Y) % N_Y
        x = (self.x + step * (1 - along_y) + N_X) % N_X
        return device(self.g, y, x, self.c)

    def row(self, step):
        return pl.ds((self.j + step + 4) % 4 * 24, self.cap)

    def block(self, step):
        return pl.ds((self.i + step + 4) % 4 * 6, 6)

    def sibling(self):
        return device(self.g, self.y, self.x, 1 - self.c)

    def describe(self, number, came, src, dst, target):
        return pltpu.make_async_remote_copy(
            src_ref=src,
            dst_ref=dst,
            send_sem=self.send.at[self.field, number],
            recv_sem=self.recv.at[self.field, came],
            device_id=target,
            device_id_type=MESH,
        )

    def copy(self, number, came, src, dst, target):
        one = self.describe(number, came, src, dst, target)
        one.start()
        self.started.append(one)
        self.made[number] = one

    def same(self, number, part, target):
        self.copy(number, number, part, part, target)

    def came(self, *numbers):
        for number in numbers:
            self.made[number].wait_recv()

    def write(self, pair, value, scratch):
        scratch[...] = value
        cube = value.reshape(8, 8, 8, 128)
        for half, edge in ((0, 0), (1, 7)):
            self.src[half, pair, 0] = scratch[pl.ds(edge, 64, stride=8), :].astype(BF16)
            self.src[half, pair, 1] = cube[:, edge].reshape(64, 128).astype(BF16)
            self.src[half, pair, 2] = value[edge * 64:edge * 64 + 64].astype(BF16)

    def clear(self):
        for half in range(2):
            self.rows[half, 96:97] = jnp.zeros((1, 3, 64, 128), BF16)

    def begin(self):
        sides, plane, c = pl.ds(0, 2), pl.ds(2, 1), self.c
        for half, step in ((0, N_Z - 1), (1, 1)):
            target = device((self.g + step) % N_Z, self.y, self.x, half)
            dst = self.line.at[pl.ds(self.first(half) * 6 + c * 3, 3), plane]
            self.copy(1 + half, 1 + c, self.src.at[half, :, plane], dst, target)
        dst = self.line.at[pl.ds(self.first(1 - c) * 6 + c * 3, 3), sides]
        self.copy(0, 0, self.src.at[1 - c, :, sides], dst, self.sibling())
        self.line[pl.ds(self.i * 6 + c * 3, 3), 0:2] = self.src[c, :, 0:2]

    def both_ways(self, number, part, first):
        lower, upper = (part + (slice(None), pl.ds(start, 32)) for start in (0, 32))
        ref = self.line if first else self.rows
        ahead, back = self.moved(first, 1), self.moved(first, -1)
        self.same(number, ref.at[lower], ahead)
        self.same(number + 1, ref.at[upper], back)
        self.same(number + 2, ref.at[upper], ahead)
        self.same(number + 3, ref.at[lower], back)

    def step0(self):
        self.came(0)
        part = self.line.at[pl.ds(0, 3), pl.ds(2, 1)]
        for core in range(2):
            self.describe(1, 1 + core, part, part, self.sibling()).wait_recv()
        self.both_ways(3, (self.block(0),), True)

    def step1(self):
        for number, step, start in ((7, 1, 0), (8, -1, 32)):
            self.came(number - 4)
            part = self.line.at[self.block(-step), :, pl.ds(start, 32)]
            self.same(number, part, self.moved(True, step))

    def step2(self):
        self.came(5, 6, 7, 8)

        def one(k, carry):
            at = self.j * 24 + k
            self.rows[self.c, at, 0:2] = self.line[self.list_ref[k, 0], 0:2]
            self.rows[self.c, at, 2:3] = self.line[self.list_ref[k, 1], 2:3]
            return carry

        lax.fori_loop(0, self.cap, one, 0)
        self.both_ways(9, (self.c, self.row(0)), False)
        self.same(15, self.rows.at[self.c, self.row(0)], self.sibling())

    def step3(self):
        for number, step, start in ((13, 1, 0), (14, -1, 32)):
            self.came(number - 4)
            part = self.rows.at[self.c, self.row(-step), :, pl.ds(start, 32)]
            self.same(number, part, self.moved(False, step))

    def step4(self):
        for number, step in ((16, 1), (17, -1)):
            self.came(number - 5)
            self.same(number, self.rows.at[self.c, self.row(-step)], self.sibling())

    def step5(self):
        for number, start in ((13, 0), (14, 32)):
            self.came(number)
            part = self.rows.at[self.c, self.row(2), :, pl.ds(start, 32)]
            self.same(number + 5, part, self.sibling())

    def step6(self):
        self.came(15, 16, 17, 18, 19)


def build_cube(cube, own, rows_ref, pos_ref, par_ref, pair):
    low = lax.broadcasted_iota(jnp.int32, (1, 128), 1) < 64
    cube[1:9, 1:9, 8:16, :] = own.reshape(8, 8, 8, 128)
    for k, (dz, dy, dx) in enumerate(DIRECTIONS):
        half, face = face_of((dz, dy, dx))
        if dz != 0 and dy != 0:
            start, count = (0, 16) if dy == 1 else (48, 16)
        else:
            start, count = 0, 64
        picked = []
        for s in range(2):
            at = pos_ref[2 * pair + s, k]
            value = rows_ref[half, at, face, start:start + count].astype(F32)
            turned = pltpu.roll(value, 64, 1)
            picked.append(jnp.where(par_ref[2 * pair + s, k] == s, value, turned))
        piece = jnp.where(low, picked[0], picked[1])
        if count == 16:
            piece = piece[0:8] if dy == 1 else piece[8:16]
        zz = {-1: 0, 1: 9}.get(dz)
        yy = {-1: 0, 1: 9}.get(dy)
        if dx == 0:
            if dz == 0:
                cube[1:9, yy, 8:16, :] = piece.reshape(8, 8, 128)
            elif dy == 0:
                cube[zz, 1:9, 8:16, :] = piece.reshape(8, 8, 128)
            else:
                cube[zz, yy, 8:16, :] = piece
            continue
        sub = 7 if dx == -1 else 16
        edge_x = 7 if dx == -1 else 0
        edge_y = 7 if dy == -1 else 0
        if dz == 0 and dy == 0:
            rows = [(z + 1, q + 1, z * 8 + q) for z in range(8) for q in range(8)]
        elif dz == 0:
            rows = [(z + 1, yy, z * 8 + edge_y) for z in range(8)]
        elif dy == 0:
            rows = [(zz, q + 1, q * 8 + edge_x) for q in range(8)]
        else:
            rows = [(zz, yy, edge_x)]
        for a, b, r in rows:
            cube[a, b, sub:sub + 1, :] = piece[r:r + 1]


def stack_taps(cube, taps, pair):
    for ty in range(3):
        for tx in range(3):
            part = cube[:, ty:ty + 8, 7 + tx:15 + tx, :].reshape(640, 128)
            column = (ty * 3 + tx) * 128
            taps[pair, :, column:column + 128] = part.astype(BF16)


def tap_of(w_ref, tap):
    value = w_ref[tap].astype(F32)
    return jnp.concatenate([value, value], axis=1)


def widen(w_ref, wide, backward):
    low = lax.broadcasted_iota(jnp.int32, (1, 128), 1) < 64
    for tz in range(3):
        for q in range(9):
            tap = tz * 9 + q
            value = tap_of(w_ref, 26 - tap if backward else tap)
            a, b = (q, tz) if backward else (tz, q)
            lanes = pl.ds(b * 128, 128)
            wide[pl.ds(a * 128, 64), lanes] = jnp.where(low, value, 0.0).astype(BF16)
            wide[pl.ds(a * 128 + 64, 64), lanes] = jnp.where(low, 0.0, value).astype(BF16)


def convolve(taps, wide, backward=False):
    contract = (((1,), (0 if backward else 1,)), ((), ()))
    wide = lax.dot_general(taps, wide[...], contract, preferred_element_type=F32)
    return wide[0:512, 0:128] + wide[64:576, 128:256] + wide[128:640, 256:384]


def spread(wide_g, pair, value):
    for tz in range(3):
        wide_g[pair, tz * 64:tz * 64 + 512, tz * 128:tz * 128 + 128] = value


def outer(wide_g, taps):
    return lax.dot_general(
        wide_g[...].reshape(PAIRS * 640, 384),
        taps[...].reshape(PAIRS * 640, 1152),
        (((0,), (0,)), ((), ())),
        preferred_element_type=F32,
    )


def block_kernel(cap, count_ref, list_ref, pos_ref, par_ref, f_ref, c_ref, w_ref, v_ref,
                 o_out, grads_out,
                 rows_x, rows_g, rows_h, line_x, line_g, line_h, src_x, src_g, src_h, xs, gs, hs, scratch, cube, taps,
                 taps_g, wide_g, wide_w, wide_b, wide_v, product, p_sum,
                 r1, a1, r2, r4, whole, send, recv, send_sum, recv_sum):
    g, y, x, c = place()
    sibling = device(g, y, x, 1 - c)
    layer = [
        ((y + ky) % N_Y, (x + kx) % N_X, ky * N_X + kx)
        for ky in range(N_Y)
        for kx in range(N_X)
        if (ky, kx) != (0, 0)
    ]
    zs = [device((g + k) % N_Z, y, x, c) for k in range(1, N_Z)]
    partners = [sibling] + [device(g, yy, xx, c) for yy, xx, _ in layer] + zs
    partners += [device((g + k) % N_Z, y, x, 1 - c) for k in (1, N_Z - 1)]
    barrier = pltpu.get_barrier_semaphore()
    for partner in partners:
        pl.semaphore_signal(barrier, inc=1, device_id=partner, device_id_type=MESH)

    count = count_ref[g, lax.axis_index("dev")]
    low = lax.broadcasted_iota(jnp.int32, (1, 128), 1) < 64
    started = []
    gx = Gather(0, cap, list_ref, rows_x, line_x, src_x, send, recv, started)
    gg = Gather(1, cap, list_ref, rows_g, line_g, src_g, send, recv, started)
    gh = Gather(2, cap, list_ref, rows_h, line_h, src_h, send, recv, started)

    def live(pair):
        return jnp.where(low, 2 * pair, 2 * pair + 1) < count

    def over_pairs(body):
        def step(pair, carry):
            body(pair)
            return carry

        lax.fori_loop(0, PAIRS, step, 0)

    def pack_x(pair):
        value = f_ref[pair].astype(F32).T
        xs[pair] = value.astype(BF16)
        gx.write(pair, value, scratch)

    def pack_g(pair):
        value = jnp.where(live(pair), c_ref[pair].astype(F32).T, 0.0)
        gs[pair] = value.astype(BF16)
        gg.write(pair, value, scratch)

    def forward(pair):
        build_cube(cube, xs[pair].astype(F32), rows_x, pos_ref, par_ref, pair)
        stack_taps(cube, taps, pair)
        first = convolve(taps[pair], wide_w)
        hidden = jnp.where(live(pair), jnp.maximum(first, 0.0), 0.0)
        hidden = hidden.astype(BF16).astype(F32)
        hs[pair] = hidden.astype(BF16)
        gh.write(pair, hidden, scratch)

    def backward(pair):
        build_cube(cube, gs[pair].astype(F32), rows_g, pos_ref, par_ref, pair)
        stack_taps(cube, taps_g, 0)
        back = convolve(taps_g[0], wide_b, True)
        grad = jnp.where(hs[pair].astype(F32) > 0, back, 0.0)
        spread(wide_g, pair, grad.astype(BF16))

    def stack_h(pair):
        build_cube(cube, hs[pair].astype(F32), rows_h, pos_ref, par_ref, pair)
        stack_taps(cube, taps, pair)
        spread(wide_g, pair, gs[pair])

    def finish(pair):
        second = convolve(taps[pair], wide_v)
        lane = lax.broadcasted_iota(jnp.int32, (128, 1), 0)
        slot = jnp.where(lane < 64, 2 * pair, 2 * pair + 1)
        result = f_ref[pair].astype(F32) + second.T
        o_out[pair] = jnp.where(slot < count, result, 0.0).astype(BF16)

    over_pairs(pack_x)
    pl.semaphore_wait(barrier, len(partners))
    gx.begin()
    for one in (gx, gg, gh):
        one.clear()
    gx.step0()
    over_pairs(pack_g)
    gx.step1()
    gg.begin()
    widen(w_ref, wide_w, False)
    gx.step2()
    gg.step0()
    widen(v_ref, wide_b, True)
    gx.step3()
    gg.step1()
    widen(v_ref, wide_v, False)
    wide_g[...] = jnp.zeros((PAIRS, 640, 384), BF16)
    gx.step4()
    gx.step5()
    gg.step2()
    gx.step6()
    over_pairs(forward)
    gh.begin()
    gg.step3()
    gh.step0()
    gh.step1()
    gg.step4()
    gh.step2()
    gg.step5()
    gg.step6()
    over_pairs(backward)
    gh.step3()
    gh.step4()
    product[...] = outer(wide_g, taps)
    for q in range(9):
        for tz in range(3):
            even, odd = pl.ds(tz * 128, 64), pl.ds(tz * 128 + 64, 64)
            lanes = pl.ds(q * 128, 128)
            one = product[even, lanes] + pltpu.roll(product[odd, lanes], 64, 1)
            p_sum[pl.ds((q * 3 + tz) * 64, 64), :] = one
    p_sum[1728:2048, :] = jnp.zeros((320, 128), F32)
    gh.step5()
    gh.step6()
    over_pairs(stack_h)
    product[...] = outer(wide_g, taps)
    for q in range(9):
        for tz in range(3):
            even, odd = pl.ds(tz * 128, 64), pl.ds(tz * 128 + 64, 64)
            lanes = pl.ds(q * 128, 128)
            rows = pl.ds((q * 3 + tz) * 64, 64)
            two = pltpu.roll(product[even, lanes], 64, 1) + product[odd, lanes]
            p_sum[rows, :] = jnp.where(low, p_sum[rows, :], two)

    used = [0]

    def copy(src, dst, target):
        number = used[0]
        used[0] += 1
        one = pltpu.make_async_remote_copy(
            src_ref=src, dst_ref=dst, send_sem=send_sum.at[number],
            recv_sem=recv_sum.at[number], device_id=target, device_id_type=MESH,
        )
        one.start()
        return one

    one = copy(p_sum.at[pl.ds((1 - c) * 1024, 1024)], r1, sibling)
    finish(0)
    one.wait()
    a1[...] = (p_sum[pl.ds(c * 1024, 1024)] + r1[...]).astype(BF16)

    made = [
        copy(a1.at[pl.ds((yy * N_X + xx) * 64, 64)], r2.at[k], device(g, yy, xx, c))
        for yy, xx, k in layer
    ]
    finish(1)
    for one in made:
        one.wait()
    at = y * N_X + x
    part = a1[pl.ds(at * 64, 64)].astype(F32)
    for k in range(1, 16):
        part = part + r2[k].astype(F32)
    r4[g] = part.astype(BF16)

    made = [copy(r4.at[g], r4.at[g], target) for target in zs]
    finish(2)
    for one in made:
        one.wait()
    part = r4[0].astype(F32)
    for k in range(1, N_Z):
        part = part + r4[k].astype(F32)
    rows = pl.ds(c * 1024 + at * 64, 64)
    whole[rows] = part.astype(BF16)

    made = [
        copy(whole.at[rows], whole.at[rows], device(g, yy, xx, c)) for yy, xx, _ in layer
    ]
    for one in made:
        one.wait()
    half = pl.ds(c * 1024, 1024)
    copy(whole.at[half], whole.at[half], sibling).wait()
    for q in range(9):
        for tz in range(3):
            grads_out[tz * 9 + q] = whole[pl.ds((q * 3 + tz) * 64, 64)]
    for one in started:
        one.wait_send()


def block(cap, collective_id, counts, lists, pos, parity, features, cotangent, w, v):
    smem, vmem = pl.BlockSpec(memory_space=pltpu.SMEM), pl.BlockSpec(memory_space=pltpu.VMEM)
    return pl.pallas_call(
        functools.partial(block_kernel, cap),
        in_specs=[smem] * 4 + [vmem] * 4,
        out_specs=[vmem] * 2,
        out_shape=[
            jax.ShapeDtypeStruct((PAIRS, 128, 512), BF16),
            jax.ShapeDtypeStruct((27, 64, 128), BF16),
        ],
        scratch_shapes=[pltpu.VMEM((2, 97, 3, 64, 128), BF16)] * 3
        + [pltpu.VMEM((24, 3, 64, 128), BF16)] * 3
        + [pltpu.VMEM((2, PAIRS, 3, 64, 128), BF16)] * 3
        + [pltpu.VMEM((PAIRS, 512, 128), BF16)] * 3
        + [
            pltpu.VMEM((512, 128), F32),
            pltpu.VMEM((10, 10, 24, 128), F32),
            pltpu.VMEM((PAIRS, 640, 1152), BF16),
            pltpu.VMEM((1, 640, 1152), BF16),
            pltpu.VMEM((PAIRS, 640, 384), BF16),
            pltpu.VMEM((384, 1152), BF16),
            pltpu.VMEM((1152, 384), BF16),
            pltpu.VMEM((384, 1152), BF16),
            pltpu.VMEM((384, 1152), F32),
            pltpu.VMEM((2048, 128), F32),
            pltpu.VMEM((1024, 128), F32),
            pltpu.VMEM((1024, 128), BF16),
            pltpu.VMEM((16, 64, 128), BF16),
            pltpu.VMEM((N_Z, 64, 128), BF16),
            pltpu.VMEM((2048, 128), BF16),
            pltpu.SemaphoreType.DMA((3, 20)),
            pltpu.SemaphoreType.DMA((3, 20)),
            pltpu.SemaphoreType.DMA((40,)),
            pltpu.SemaphoreType.DMA((40,)),
        ],
        compiler_params=pltpu.CompilerParams(
            collective_id=collective_id, has_side_effects=True, vmem_limit_bytes=62 * 2**20
        ),
    )(counts, lists, pos, parity, features, cotangent, w, v)


def table_kernel(counts_ref, near_ref, needed_out, list_out, pos_out, par_out):
    g, y, x, c = place()
    iota = lambda shape, dim: lax.broadcasted_iota(jnp.int32, shape, dim)
    rows = (lambda d: d >> 3, lambda d: (d >> 1) & 3)
    orders = (lambda d: (d >> 1 & 3) * 2 + (d & 1), lambda d: (d >> 3) * 2 + (d & 1))
    pairs = ((counts_ref[...] + 1) >> 1).astype(F32)
    other, this = iota((32, 32), 0), iota((32, 32), 1)
    base = []
    for half in range(2):
        before = (rows[half](other) == rows[half](this)) & (
            orders[half](other) < orders[half](this)
        )
        base.append(jnp.dot(pairs, before.astype(F32), preferred_element_type=F32))
    top = jnp.max(jnp.maximum(base[0], base[1]) + pairs)
    needed_out[0] = top.astype(jnp.int32)

    group = iota((N_Z, 32), 0)

    def of_group(value, which):
        return jnp.sum(jnp.where(group == which, value, 0.0), axis=0, keepdims=True)

    near = near_ref[...]
    owner = (near * 10923) >> 16
    within = near - 6 * owner
    dev = owner & 31
    lane, device_lane = iota((6, 26), 1), iota((6, 32), 1)
    pos = jnp.zeros((6, 26), jnp.int32)
    for k, direction in enumerate(DIRECTIONS):
        half = face_of(direction)[0]
        line = of_group(base[half], g + direction[0])
        hit = dev[:, k:k + 1] == device_lane
        rank = jnp.sum(jnp.where(hit, line, 0.0), axis=1, keepdims=True).astype(jnp.int32)
        pos = jnp.where(lane == k, rank + rows[half](dev) * 24, pos)
    pos_out[...] = jnp.where(near >= 0, pos + (within >> 1), 96)
    par_out[...] = within & 1

    lead = c == 0
    d = iota((24, 32), 1)
    own_row = jnp.where(lead, y, x)
    inside = jnp.where(lead, rows[0](d), rows[1](d)) == own_row
    order = jnp.where(lead, orders[0](d), orders[1](d))
    start = jnp.where(lead, base[0], base[1])
    for source, which in enumerate((g, (g + jnp.where(lead, 1, N_Z - 1)) % N_Z)):
        rank = of_group(start, which).astype(jnp.int32)
        size = of_group(pairs, which).astype(jnp.int32)
        found = jnp.zeros((24, 1), F32)
        for p in range(3):
            match = inside & (rank + p == iota((24, 32), 0)) & (size > p)
            found += jnp.sum(
                jnp.where(match, (order * 3 + p).astype(F32), 0.0), axis=1, keepdims=True
            )
        list_out[:, source:source + 1] = found.astype(jnp.int32)


def tables(counts, neighbours):
    vmem = pl.BlockSpec(memory_space=pltpu.VMEM)
    return pl.pallas_call(
        table_kernel,
        in_specs=[vmem] * 2,
        out_specs=[pl.BlockSpec(memory_space=pltpu.SMEM)] + [vmem] * 3,
        out_shape=[
            jax.ShapeDtypeStruct((1,), jnp.int32),
            jax.ShapeDtypeStruct((24, 2), jnp.int32),
            jax.ShapeDtypeStruct((6, 26), jnp.int32),
            jax.ShapeDtypeStruct((6, 26), jnp.int32),
        ],
    )(counts, neighbours)


def per_device(features, cotangent, first_weight, second_weight, counts, neighbours):
    needed, lists, pos, parity = tables(counts, neighbours)
    operands = (
        counts,
        lists,
        pos,
        parity,
        features.reshape(PAIRS, 128, 512),
        cotangent.reshape(PAIRS, 128, 512),
        first_weight.transpose(1, 0, 2),
        second_weight.transpose(1, 0, 2),
    )
    out, grads = lax.switch(
        sum((needed[0] > cap).astype(jnp.int32) for cap in CAPS[:-1]),
        [functools.partial(block, cap, i) for i, cap in enumerate(CAPS)],
        *operands,
    )
    return (
        out.reshape(6, 64, 512),
        grads[:, :, :64].astype(F32).transpose(1, 0, 2),
        grads[:, :, 64:].astype(F32).transpose(1, 0, 2),
    )


def solution(mesh):
    placed = (
        P(("group", "dev"), None, None),
        P(("group", "dev"), None, None),
        P(),
        P(),
        P(),
        P(("group", "dev"), None),
    )
    return jax.shard_map(
        per_device,
        mesh=mesh,
        in_specs=placed,
        out_specs=(P(("group", "dev"), None, None), P(), P()),
        check_vma=False,
    )
```

```python
import functools

import jax
import jax.numpy as jnp
import numpy as np
from jax import lax
from jax.experimental import pallas as pl
from jax.experimental.pallas import tpu as pltpu
from jax.sharding import PartitionSpec as P

MESH = pl.DeviceIdType.MESH
F32 = jnp.float32
BF16 = jnp.bfloat16
N_Z, N_Y, N_X = 8, 4, 4
PAIRS = 3
CAPS = (14, 16, 24)
DIRECTIONS = [
    (dz, dy, dx)
    for dz in (-1, 0, 1)
    for dy in (-1, 0, 1)
    for dx in (-1, 0, 1)
    if (dz, dy, dx) != (0, 0, 0)
]


def face_of(direction):
    dz, dy, dx = direction
    if dz != 0:
        return (0 if dz == 1 else 1), 2
    if dx != 0:
        return (0 if dx == 1 else 1), 0
    return (0 if dy == 1 else 1), 1


def place():
    d = lax.axis_index("dev")
    return lax.axis_index("group"), d // 8, (d // 2) % 4, d % 2


def device(g, y, x, c):
    return (g, (y * 4 + x) * 2 + c)


class Gather:
    def __init__(self, field, cap, list_ref, rows, line, src, send, recv, started):
        self.field, self.cap, self.list_ref = field, cap, list_ref
        self.rows, self.line, self.src = rows, line, src
        self.send, self.recv, self.started = send, recv, started
        self.g, self.y, self.x, self.c = place()
        self.i = self.first(self.c)
        self.j = self.first(1 - self.c)
        self.made = dict()

    def first(self, half):
        return self.x * (1 - half) + self.y * half

    def moved(self, first, step):
        along_y = self.c if first else 1 - self.c
        y = (self.y + step * along_y + N_Y) % N_Y
        x = (self.x + step * (1 - along_y) + N_X) % N_X
        return device(self.g, y, x, self.c)

    def row(self, step):
        return pl.ds((self.j + step + 4) % 4 * 24, self.cap)

    def block(self, step):
        return pl.ds((self.i + step + 4) % 4 * 6, 6)

    def sibling(self):
        return device(self.g, self.y, self.x, 1 - self.c)

    def describe(self, number, came, src, dst, target):
        return pltpu.make_async_remote_copy(
            src_ref=src,
            dst_ref=dst,
            send_sem=self.send.at[self.field, number],
            recv_sem=self.recv.at[self.field, came],
            device_id=target,
            device_id_type=MESH,
        )

    def copy(self, number, came, src, dst, target):
        one = self.describe(number, came, src, dst, target)
        one.start()
        self.started.append(one)
        self.made[number] = one

    def same(self, number, part, target):
        self.copy(number, number, part, part, target)

    def came(self, *numbers):
        for number in numbers:
            self.made[number].wait_recv()

    def write(self, pair, value, scratch):
        scratch[...] = value
        cube = value.reshape(8, 8, 8, 128)
        for half, edge in ((0, 0), (1, 7)):
            self.src[half, pair, 0] = scratch[pl.ds(edge, 64, stride=8), :].astype(BF16)
            self.src[half, pair, 1] = cube[:, edge].reshape(64, 128).astype(BF16)
            self.src[half, pair, 2] = value[edge * 64:edge * 64 + 64].astype(BF16)

    def clear(self):
        for half in range(2):
            self.rows[half, 96:97] = jnp.zeros((1, 3, 64, 128), BF16)

    def begin(self):
        sides, plane, c = pl.ds(0, 2), pl.ds(2, 1), self.c
        for half, step in ((0, N_Z - 1), (1, 1)):
            target = device((self.g + step) % N_Z, self.y, self.x, half)
            dst = self.line.at[pl.ds(self.first(half) * 6 + c * 3, 3), plane]
            self.copy(1 + half, 1 + c, self.src.at[half, :, plane], dst, target)
        dst = self.line.at[pl.ds(self.first(1 - c) * 6 + c * 3, 3), sides]
        self.copy(0, 0, self.src.at[1 - c, :, sides], dst, self.sibling())
        self.line[pl.ds(self.i * 6 + c * 3, 3), 0:2] = self.src[c, :, 0:2]

    def both_ways(self, number, part, first):
        lower, upper = (part + (slice(None), pl.ds(start, 32)) for start in (0, 32))
        ref = self.line if first else self.rows
        ahead, back = self.moved(first, 1), self.moved(first, -1)
        self.same(number, ref.at[lower], ahead)
        self.same(number + 1, ref.at[upper], back)
        self.same(number + 2, ref.at[upper], ahead)
        self.same(number + 3, ref.at[lower], back)

    def step0(self):
        self.came(0)
        part = self.line.at[pl.ds(0, 3), pl.ds(2, 1)]
        for core in range(2):
            self.describe(1, 1 + core, part, part, self.sibling()).wait_recv()
        self.both_ways(3, (self.block(0),), True)

    def step1(self):
        for number, step, start in ((7, 1, 0), (8, -1, 32)):
            self.came(number - 4)
            part = self.line.at[self.block(-step), :, pl.ds(start, 32)]
            self.same(number, part, self.moved(True, step))

    def step2(self):
        self.came(5, 6, 7, 8)

        def one(k, carry):
            at = self.j * 24 + k
            self.rows[self.c, at, 0:2] = self.line[self.list_ref[k, 0], 0:2]
            self.rows[self.c, at, 2:3] = self.line[self.list_ref[k, 1], 2:3]
            return carry

        lax.fori_loop(0, self.cap, one, 0)
        self.both_ways(9, (self.c, self.row(0)), False)
        self.same(15, self.rows.at[self.c, self.row(0)], self.sibling())

    def step3(self):
        for number, step, start in ((13, 1, 0), (14, -1, 32)):
            self.came(number - 4)
            part = self.rows.at[self.c, self.row(-step), :, pl.ds(start, 32)]
            self.same(number, part, self.moved(False, step))

    def step4(self):
        for number, step in ((16, 1), (17, -1)):
            self.came(number - 5)
            self.same(number, self.rows.at[self.c, self.row(-step)], self.sibling())

    def step5(self):
        for number, start in ((13, 0), (14, 32)):
            self.came(number)
            part = self.rows.at[self.c, self.row(2), :, pl.ds(start, 32)]
            self.same(number + 5, part, self.sibling())

    def step6(self):
        self.came(15, 16, 17, 18, 19)


def build_cube(cube, own, rows_ref, pos_ref, par_ref, pair):
    low = lax.broadcasted_iota(jnp.int32, (1, 128), 1) < 64
    cube[1:9, 1:9, 8:16, :] = own.reshape(8, 8, 8, 128)
    for k, (dz, dy, dx) in enumerate(DIRECTIONS):
        half, face = face_of((dz, dy, dx))
        if dz != 0 and dy != 0:
            start, count = (0, 16) if dy == 1 else (48, 16)
        else:
            start, count = 0, 64
        picked = []
        for s in range(2):
            at = pos_ref[2 * pair + s, k]
            value = rows_ref[half, at, face, start:start + count].astype(F32)
            turned = pltpu.roll(value, 64, 1)
            picked.append(jnp.where(par_ref[2 * pair + s, k] == s, value, turned))
        piece = jnp.where(low, picked[0], picked[1])
        if count == 16:
            piece = piece[0:8] if dy == 1 else piece[8:16]
        zz = {-1: 0, 1: 9}.get(dz)
        yy = {-1: 0, 1: 9}.get(dy)
        if dx == 0:
            if dz == 0:
                cube[1:9, yy, 8:16, :] = piece.reshape(8, 8, 128)
            elif dy == 0:
                cube[zz, 1:9, 8:16, :] = piece.reshape(8, 8, 128)
            else:
                cube[zz, yy, 8:16, :] = piece
            continue
        sub = 7 if dx == -1 else 16
        edge_x = 7 if dx == -1 else 0
        edge_y = 7 if dy == -1 else 0
        if dz == 0 and dy == 0:
            rows = [(z + 1, q + 1, z * 8 + q) for z in range(8) for q in range(8)]
        elif dz == 0:
            rows = [(z + 1, yy, z * 8 + edge_y) for z in range(8)]
        elif dy == 0:
            rows = [(zz, q + 1, q * 8 + edge_x) for q in range(8)]
        else:
            rows = [(zz, yy, edge_x)]
        for a, b, r in rows:
            cube[a, b, sub:sub + 1, :] = piece[r:r + 1]


def stack_taps(cube, taps, pair):
    for ty in range(3):
        for tx in range(3):
            part = cube[:, ty:ty + 8, 7 + tx:15 + tx, :].reshape(640, 128)
            column = (ty * 3 + tx) * 128
            taps[pair, :, column:column + 128] = part.astype(BF16)


def tap_of(w_ref, tap):
    value = w_ref[tap].astype(F32)
    return jnp.concatenate([value, value], axis=1)


def widen(w_ref, wide, backward):
    low = lax.broadcasted_iota(jnp.int32, (1, 128), 1) < 64
    for tz in range(3):
        for q in range(9):
            tap = tz * 9 + q
            value = tap_of(w_ref, 26 - tap if backward else tap)
            a, b = (q, tz) if backward else (tz, q)
            lanes = pl.ds(b * 128, 128)
            wide[pl.ds(a * 128, 64), lanes] = jnp.where(low, value, 0.0).astype(BF16)
            wide[pl.ds(a * 128 + 64, 64), lanes] = jnp.where(low, 0.0, value).astype(BF16)


def convolve(taps, wide, backward=False):
    contract = (((1,), (0 if backward else 1,)), ((), ()))
    wide = lax.dot_general(taps, wide[...], contract, preferred_element_type=F32)
    return wide[0:512, 0:128] + wide[64:576, 128:256] + wide[128:640, 256:384]


def spread(wide_g, pair, value):
    for tz in range(3):
        wide_g[pair, tz * 64:tz * 64 + 512, tz * 128:tz * 128 + 128] = value


def outer(one, other):
    return lax.dot_general(
        one[...].reshape(PAIRS * 640, one.shape[2]),
        other[...].reshape(PAIRS * 640, other.shape[2]),
        (((0,), (0,)), ((), ())),
        preferred_element_type=F32,
    )


def block_kernel(cap, count_ref, list_ref, pos_ref, par_ref, f_ref, c_ref, w_ref, v_ref,
                 o_out, grads_out,
                 rows_x, rows_g, rows_h, line_x, line_g, line_h, src_x, src_g, src_h, xs, gs, hs, scratch, cube, taps,
                 taps_g, wide_g, wide_w, wide_b, wide_v, product, product_g, p_sum,
                 r1, a1, r2, r4, whole, send, recv, send_sum, recv_sum):
    g, y, x, c = place()
    sibling = device(g, y, x, 1 - c)
    layer = [
        ((y + ky) % N_Y, (x + kx) % N_X, ky * N_X + kx)
        for ky in range(N_Y)
        for kx in range(N_X)
        if (ky, kx) != (0, 0)
    ]
    zs = [device((g + k) % N_Z, y, x, c) for k in range(1, N_Z)]
    partners = [sibling] + [device(g, yy, xx, c) for yy, xx, _ in layer] + zs
    partners += [device((g + k) % N_Z, y, x, 1 - c) for k in (1, N_Z - 1)]
    barrier = pltpu.get_barrier_semaphore()
    for partner in partners:
        pl.semaphore_signal(barrier, inc=1, device_id=partner, device_id_type=MESH)

    count = count_ref[g, lax.axis_index("dev")]
    low = lax.broadcasted_iota(jnp.int32, (1, 128), 1) < 64
    started = []
    gx = Gather(0, cap, list_ref, rows_x, line_x, src_x, send, recv, started)
    gg = Gather(1, cap, list_ref, rows_g, line_g, src_g, send, recv, started)
    gh = Gather(2, cap, list_ref, rows_h, line_h, src_h, send, recv, started)

    def live(pair):
        return jnp.where(low, 2 * pair, 2 * pair + 1) < count

    def over_pairs(body):
        def step(pair, carry):
            body(pair)
            return carry

        lax.fori_loop(0, PAIRS, step, 0)

    def pack_x(pair):
        value = f_ref[pair].astype(F32).T
        xs[pair] = value.astype(BF16)
        gx.write(pair, value, scratch)

    def pack_g(pair):
        value = jnp.where(live(pair), c_ref[pair].astype(F32).T, 0.0)
        gs[pair] = value.astype(BF16)
        gg.write(pair, value, scratch)

    def forward(pair):
        build_cube(cube, xs[pair].astype(F32), rows_x, pos_ref, par_ref, pair)
        stack_taps(cube, taps, pair)
        first = convolve(taps[pair], wide_w)
        hidden = jnp.where(live(pair), jnp.maximum(first, 0.0), 0.0)
        hidden = hidden.astype(BF16).astype(F32)
        hs[pair] = hidden.astype(BF16)
        gh.write(pair, hidden, scratch)

    def backward(pair):
        build_cube(cube, gs[pair].astype(F32), rows_g, pos_ref, par_ref, pair)
        stack_taps(cube, taps_g, pair)
        back = convolve(taps_g[pair], wide_b, True)
        grad = jnp.where(hs[pair].astype(F32) > 0, back, 0.0)
        spread(wide_g, pair, grad.astype(BF16))

    def finish(pair):
        build_cube(cube, hs[pair].astype(F32), rows_h, pos_ref, par_ref, pair)
        stack_taps(cube, taps, pair)
        second = convolve(taps[pair], wide_v)
        lane = lax.broadcasted_iota(jnp.int32, (128, 1), 0)
        slot = jnp.where(lane < 64, 2 * pair, 2 * pair + 1)
        result = f_ref[pair].astype(F32) + second.T
        o_out[pair] = jnp.where(slot < count, result, 0.0).astype(BF16)

    over_pairs(pack_x)
    pl.semaphore_wait(barrier, len(partners))
    gx.begin()
    for one in (gx, gg, gh):
        one.clear()
    gx.step0()
    over_pairs(pack_g)
    gx.step1()
    gg.begin()
    widen(w_ref, wide_w, False)
    gx.step2()
    gg.step0()
    widen(v_ref, wide_b, True)
    gx.step3()
    gg.step1()
    widen(v_ref, wide_v, False)
    wide_g[...] = jnp.zeros((PAIRS, 640, 384), BF16)
    gx.step4()
    gx.step5()
    gg.step2()
    gx.step6()
    over_pairs(forward)
    gh.begin()
    gg.step3()
    gh.step0()
    gh.step1()
    gg.step4()
    gg.step5()
    gh.step2()
    gg.step6()
    over_pairs(backward)
    gh.step3()
    product[...] = outer(wide_g, taps)
    gh.step4()
    for q in range(9):
        for tz in range(3):
            even, odd = pl.ds(tz * 128, 64), pl.ds(tz * 128 + 64, 64)
            lanes = pl.ds(q * 128, 128)
            one = product[even, lanes] + pltpu.roll(product[odd, lanes], 64, 1)
            p_sum[pl.ds((q * 3 + tz) * 64, 64), :] = one
    p_sum[1728:2048, :] = jnp.zeros((320, 128), F32)
    over_pairs(lambda pair: spread(wide_g, pair, hs[pair]))
    product_g[...] = outer(taps_g, wide_g)
    for q in range(9):
        for tz in range(3):
            even, odd = pl.ds((8 - q) * 128, 64), pl.ds((8 - q) * 128 + 64, 64)
            lanes = pl.ds((2 - tz) * 128, 128)
            rows = pl.ds((q * 3 + tz) * 64, 64)
            two = pltpu.roll(product_g[even, lanes], 64, 1) + product_g[odd, lanes]
            p_sum[rows, :] = jnp.where(low, p_sum[rows, :], two)

    used = [0]

    def copy(src, dst, target):
        number = used[0]
        used[0] += 1
        one = pltpu.make_async_remote_copy(
            src_ref=src, dst_ref=dst, send_sem=send_sum.at[number],
            recv_sem=recv_sum.at[number], device_id=target, device_id_type=MESH,
        )
        one.start()
        return one

    one = copy(p_sum.at[pl.ds((1 - c) * 1024, 1024)], r1, sibling)
    gh.step5()
    one.wait()
    a1[...] = (p_sum[pl.ds(c * 1024, 1024)] + r1[...]).astype(BF16)

    made = [
        copy(a1.at[pl.ds((yy * N_X + xx) * 64, 64)], r2.at[k], device(g, yy, xx, c))
        for yy, xx, k in layer
    ]
    gh.step6()
    finish(0)
    for one in made:
        one.wait()
    at = y * N_X + x
    part = a1[pl.ds(at * 64, 64)].astype(F32)
    for k in range(1, 16):
        part = part + r2[k].astype(F32)
    r4[g] = part.astype(BF16)

    made = [copy(r4.at[g], r4.at[g], target) for target in zs]
    finish(1)
    for one in made:
        one.wait()
    part = r4[0].astype(F32)
    for k in range(1, N_Z):
        part = part + r4[k].astype(F32)
    rows = pl.ds(c * 1024 + at * 64, 64)
    whole[rows] = part.astype(BF16)

    made = [
        copy(whole.at[rows], whole.at[rows], device(g, yy, xx, c)) for yy, xx, _ in layer
    ]
    finish(2)
    for one in made:
        one.wait()
    half = pl.ds(c * 1024, 1024)
    copy(whole.at[half], whole.at[half], sibling).wait()
    for q in range(9):
        for tz in range(3):
            grads_out[tz * 9 + q] = whole[pl.ds((q * 3 + tz) * 64, 64)]
    for one in started:
        one.wait_send()


def block(cap, collective_id, counts, lists, pos, parity, features, cotangent, w, v):
    smem, vmem = pl.BlockSpec(memory_space=pltpu.SMEM), pl.BlockSpec(memory_space=pltpu.VMEM)
    return pl.pallas_call(
        functools.partial(block_kernel, cap),
        in_specs=[smem] * 4 + [vmem] * 4,
        out_specs=[vmem] * 2,
        out_shape=[
            jax.ShapeDtypeStruct((PAIRS, 128, 512), BF16),
            jax.ShapeDtypeStruct((27, 64, 128), BF16),
        ],
        scratch_shapes=[pltpu.VMEM((2, 97, 3, 64, 128), BF16)] * 3
        + [pltpu.VMEM((24, 3, 64, 128), BF16)] * 3
        + [pltpu.VMEM((2, PAIRS, 3, 64, 128), BF16)] * 3
        + [pltpu.VMEM((PAIRS, 512, 128), BF16)] * 3
        + [
            pltpu.VMEM((512, 128), F32),
            pltpu.VMEM((10, 10, 24, 128), F32),
            pltpu.VMEM((PAIRS, 640, 1152), BF16),
            pltpu.VMEM((PAIRS, 640, 1152), BF16),
            pltpu.VMEM((PAIRS, 640, 384), BF16),
            pltpu.VMEM((384, 1152), BF16),
            pltpu.VMEM((1152, 384), BF16),
            pltpu.VMEM((384, 1152), BF16),
            pltpu.VMEM((384, 1152), F32),
            pltpu.VMEM((1152, 384), F32),
            pltpu.VMEM((2048, 128), F32),
            pltpu.VMEM((1024, 128), F32),
            pltpu.VMEM((1024, 128), BF16),
            pltpu.VMEM((16, 64, 128), BF16),
            pltpu.VMEM((N_Z, 64, 128), BF16),
            pltpu.VMEM((2048, 128), BF16),
            pltpu.SemaphoreType.DMA((3, 20)),
            pltpu.SemaphoreType.DMA((3, 20)),
            pltpu.SemaphoreType.DMA((40,)),
            pltpu.SemaphoreType.DMA((40,)),
        ],
        compiler_params=pltpu.CompilerParams(
            collective_id=collective_id, has_side_effects=True, vmem_limit_bytes=62 * 2**20
        ),
    )(counts, lists, pos, parity, features, cotangent, w, v)


def table_kernel(counts_ref, near_ref, needed_out, list_out, pos_out, par_out):
    g, y, x, c = place()
    iota = lambda shape, dim: lax.broadcasted_iota(jnp.int32, shape, dim)
    rows = (lambda d: d >> 3, lambda d: (d >> 1) & 3)
    orders = (lambda d: (d >> 1 & 3) * 2 + (d & 1), lambda d: (d >> 3) * 2 + (d & 1))
    pairs = ((counts_ref[...] + 1) >> 1).astype(F32)
    other, this = iota((32, 32), 0), iota((32, 32), 1)
    base = []
    for half in range(2):
        before = (rows[half](other) == rows[half](this)) & (
            orders[half](other) < orders[half](this)
        )
        base.append(jnp.dot(pairs, before.astype(F32), preferred_element_type=F32))
    top = jnp.max(jnp.maximum(base[0], base[1]) + pairs)
    needed_out[0] = top.astype(jnp.int32)

    group = iota((N_Z, 32), 0)

    def of_group(value, which):
        return jnp.sum(jnp.where(group == which, value, 0.0), axis=0, keepdims=True)

    near = near_ref[...]
    owner = (near * 10923) >> 16
    within = near - 6 * owner
    dev = owner & 31
    lane, device_lane = iota((6, 26), 1), iota((6, 32), 1)
    pos = jnp.zeros((6, 26), jnp.int32)
    for k, direction in enumerate(DIRECTIONS):
        half = face_of(direction)[0]
        line = of_group(base[half], g + direction[0])
        hit = dev[:, k:k + 1] == device_lane
        rank = jnp.sum(jnp.where(hit, line, 0.0), axis=1, keepdims=True).astype(jnp.int32)
        pos = jnp.where(lane == k, rank + rows[half](dev) * 24, pos)
    pos_out[...] = jnp.where(near >= 0, pos + (within >> 1), 96)
    par_out[...] = within & 1

    lead = c == 0
    d = iota((24, 32), 1)
    own_row = jnp.where(lead, y, x)
    inside = jnp.where(lead, rows[0](d), rows[1](d)) == own_row
    order = jnp.where(lead, orders[0](d), orders[1](d))
    start = jnp.where(lead, base[0], base[1])
    for source, which in enumerate((g, (g + jnp.where(lead, 1, N_Z - 1)) % N_Z)):
        rank = of_group(start, which).astype(jnp.int32)
        size = of_group(pairs, which).astype(jnp.int32)
        found = jnp.zeros((24, 1), F32)
        for p in range(3):
            match = inside & (rank + p == iota((24, 32), 0)) & (size > p)
            found += jnp.sum(
                jnp.where(match, (order * 3 + p).astype(F32), 0.0), axis=1, keepdims=True
            )
        list_out[:, source:source + 1] = found.astype(jnp.int32)


def tables(counts, neighbours):
    vmem = pl.BlockSpec(memory_space=pltpu.VMEM)
    return pl.pallas_call(
        table_kernel,
        in_specs=[vmem] * 2,
        out_specs=[pl.BlockSpec(memory_space=pltpu.SMEM)] + [vmem] * 3,
        out_shape=[
            jax.ShapeDtypeStruct((1,), jnp.int32),
            jax.ShapeDtypeStruct((24, 2), jnp.int32),
            jax.ShapeDtypeStruct((6, 26), jnp.int32),
            jax.ShapeDtypeStruct((6, 26), jnp.int32),
        ],
    )(counts, neighbours)


def per_device(features, cotangent, first_weight, second_weight, counts, neighbours):
    needed, lists, pos, parity = tables(counts, neighbours)
    operands = (
        counts,
        lists,
        pos,
        parity,
        features.reshape(PAIRS, 128, 512),
        cotangent.reshape(PAIRS, 128, 512),
        first_weight.transpose(1, 0, 2),
        second_weight.transpose(1, 0, 2),
    )
    out, grads = lax.switch(
        sum((needed[0] > cap).astype(jnp.int32) for cap in CAPS[:-1]),
        [functools.partial(block, cap, i) for i, cap in enumerate(CAPS)],
        *operands,
    )
    return (
        out.reshape(6, 64, 512),
        grads[:, :, :64].astype(F32).transpose(1, 0, 2),
        grads[:, :, 64:].astype(F32).transpose(1, 0, 2),
    )


def solution(mesh):
    placed = (
        P(("group", "dev"), None, None),
        P(("group", "dev"), None, None),
        P(),
        P(),
        P(),
        P(("group", "dev"), None),
    )
    return jax.shard_map(
        per_device,
        mesh=mesh,
        in_specs=placed,
        out_specs=(P(("group", "dev"), None, None), P(), P()),
        check_vma=False,
    )
```

```python
import functools

import jax
import jax.numpy as jnp
import numpy as np
from jax import lax
from jax.experimental import pallas as pl
from jax.experimental.pallas import tpu as pltpu
from jax.sharding import PartitionSpec as P

MESH = pl.DeviceIdType.MESH
F32 = jnp.float32
BF16 = jnp.bfloat16
N_Z, N_Y, N_X = 8, 4, 4
PAIRS = 3
CAPS = (14, 16, 24)
DIRECTIONS = [
    (dz, dy, dx)
    for dz in (-1, 0, 1)
    for dy in (-1, 0, 1)
    for dx in (-1, 0, 1)
    if (dz, dy, dx) != (0, 0, 0)
]


def face_of(direction):
    dz, dy, dx = direction
    if dz != 0:
        return (0 if dz == 1 else 1), 2
    if dx != 0:
        return (0 if dx == 1 else 1), 0
    return (0 if dy == 1 else 1), 1


def place():
    d = lax.axis_index("dev")
    return lax.axis_index("group"), d // 8, (d // 2) % 4, d % 2


def device(g, y, x, c):
    return (g, (y * 4 + x) * 2 + c)


class Gather:
    def __init__(self, field, cap, list_ref, rows, line, src, send, recv, started):
        self.field, self.cap, self.list_ref = field, cap, list_ref
        self.rows, self.line, self.src = rows, line, src
        self.send, self.recv, self.started = send, recv, started
        self.g, self.y, self.x, self.c = place()
        self.i = self.first(self.c)
        self.j = self.first(1 - self.c)
        self.made = dict()

    def first(self, half):
        return self.x * (1 - half) + self.y * half

    def moved(self, first, step):
        along_y = self.c if first else 1 - self.c
        y = (self.y + step * along_y + N_Y) % N_Y
        x = (self.x + step * (1 - along_y) + N_X) % N_X
        return device(self.g, y, x, self.c)

    def row(self, step):
        return pl.ds((self.j + step + 4) % 4 * 24, self.cap)

    def block(self, step):
        return pl.ds((self.i + step + 4) % 4 * 6, 6)

    def sibling(self):
        return device(self.g, self.y, self.x, 1 - self.c)

    def describe(self, number, came, src, dst, target):
        return pltpu.make_async_remote_copy(
            src_ref=src,
            dst_ref=dst,
            send_sem=self.send.at[self.field, number],
            recv_sem=self.recv.at[self.field, came],
            device_id=target,
            device_id_type=MESH,
        )

    def copy(self, number, came, src, dst, target):
        one = self.describe(number, came, src, dst, target)
        one.start()
        self.started.append(one)
        self.made[number] = one

    def same(self, number, part, target):
        self.copy(number, number, part, part, target)

    def came(self, *numbers):
        for number in numbers:
            self.made[number].wait_recv()

    def write(self, pair, value, scratch):
        scratch[...] = value
        cube = value.reshape(8, 8, 8, 128)
        for half, edge in ((0, 0), (1, 7)):
            self.src[half, pair, 0] = scratch[pl.ds(edge, 64, stride=8), :].astype(BF16)
            self.src[half, pair, 1] = cube[:, edge].reshape(64, 128).astype(BF16)
            self.src[half, pair, 2] = value[edge * 64:edge * 64 + 64].astype(BF16)

    def clear(self):
        for half in range(2):
            self.rows[half, 96:97] = jnp.zeros((1, 3, 64, 128), BF16)

    def begin(self):
        sides, plane, c = pl.ds(0, 2), pl.ds(2, 1), self.c
        for half, step in ((0, N_Z - 1), (1, 1)):
            target = device((self.g + step) % N_Z, self.y, self.x, half)
            dst = self.line.at[pl.ds(self.first(half) * 6 + c * 3, 3), plane]
            self.copy(1 + half, 1 + c, self.src.at[half, :, plane], dst, target)
        dst = self.line.at[pl.ds(self.first(1 - c) * 6 + c * 3, 3), sides]
        self.copy(0, 0, self.src.at[1 - c, :, sides], dst, self.sibling())
        self.line[pl.ds(self.i * 6 + c * 3, 3), 0:2] = self.src[c, :, 0:2]

    def both_ways(self, number, part, first):
        lower, upper = (part + (slice(None), pl.ds(start, 32)) for start in (0, 32))
        ref = self.line if first else self.rows
        ahead, back = self.moved(first, 1), self.moved(first, -1)
        self.same(number, ref.at[lower], ahead)
        self.same(number + 1, ref.at[upper], back)
        self.same(number + 2, ref.at[upper], ahead)
        self.same(number + 3, ref.at[lower], back)

    def step0(self):
        self.came(0)
        part = self.line.at[pl.ds(0, 3), pl.ds(2, 1)]
        for core in range(2):
            self.describe(1, 1 + core, part, part, self.sibling()).wait_recv()
        self.both_ways(3, (self.block(0),), True)

    def step1(self):
        for number, step, start in ((7, 1, 0), (8, -1, 32)):
            self.came(number - 4)
            part = self.line.at[self.block(-step), :, pl.ds(start, 32)]
            self.same(number, part, self.moved(True, step))

    def step2(self):
        self.came(5, 6, 7, 8)

        def one(k, carry):
            at = self.j * 24 + k
            self.rows[self.c, at, 0:2] = self.line[self.list_ref[k, 0], 0:2]
            self.rows[self.c, at, 2:3] = self.line[self.list_ref[k, 1], 2:3]
            return carry

        lax.fori_loop(0, self.cap, one, 0)
        self.both_ways(9, (self.c, self.row(0)), False)
        self.same(15, self.rows.at[self.c, self.row(0)], self.sibling())

    def step3(self):
        for number, step, start in ((13, 1, 0), (14, -1, 32)):
            self.came(number - 4)
            part = self.rows.at[self.c, self.row(-step), :, pl.ds(start, 32)]
            self.same(number, part, self.moved(False, step))

    def step4(self):
        for number, step in ((16, 1), (17, -1)):
            self.came(number - 5)
            self.same(number, self.rows.at[self.c, self.row(-step)], self.sibling())

    def step5(self):
        for number, start in ((13, 0), (14, 32)):
            self.came(number)
            part = self.rows.at[self.c, self.row(2), :, pl.ds(start, 32)]
            self.same(number + 5, part, self.sibling())

    def step6(self):
        self.came(15, 16, 17, 18, 19)


def build_cube(cube, own, rows_ref, pos_ref, par_ref, pair):
    low = lax.broadcasted_iota(jnp.int32, (1, 128), 1) < 64
    cube[1:9, 1:9, 8:16, :] = own.reshape(8, 8, 8, 128)
    for k, (dz, dy, dx) in enumerate(DIRECTIONS):
        half, face = face_of((dz, dy, dx))
        if dz != 0 and dy != 0:
            start, count = (0, 16) if dy == 1 else (48, 16)
        else:
            start, count = 0, 64
        picked = []
        for s in range(2):
            at = pos_ref[2 * pair + s, k]
            value = rows_ref[half, at, face, start:start + count].astype(F32)
            turned = pltpu.roll(value, 64, 1)
            picked.append(jnp.where(par_ref[2 * pair + s, k] == s, value, turned))
        piece = jnp.where(low, picked[0], picked[1])
        if count == 16:
            piece = piece[0:8] if dy == 1 else piece[8:16]
        zz = {-1: 0, 1: 9}.get(dz)
        yy = {-1: 0, 1: 9}.get(dy)
        if dx == 0:
            if dz == 0:
                cube[1:9, yy, 8:16, :] = piece.reshape(8, 8, 128)
            elif dy == 0:
                cube[zz, 1:9, 8:16, :] = piece.reshape(8, 8, 128)
            else:
                cube[zz, yy, 8:16, :] = piece
            continue
        sub = 7 if dx == -1 else 16
        edge_x = 7 if dx == -1 else 0
        edge_y = 7 if dy == -1 else 0
        if dz == 0 and dy == 0:
            rows = [(z + 1, q + 1, z * 8 + q) for z in range(8) for q in range(8)]
        elif dz == 0:
            rows = [(z + 1, yy, z * 8 + edge_y) for z in range(8)]
        elif dy == 0:
            rows = [(zz, q + 1, q * 8 + edge_x) for q in range(8)]
        else:
            rows = [(zz, yy, edge_x)]
        for a, b, r in rows:
            cube[a, b, sub:sub + 1, :] = piece[r:r + 1]


def stack_taps(cube, taps, pair):
    for ty in range(3):
        for tx in range(3):
            part = cube[:, ty:ty + 8, 7 + tx:15 + tx, :].reshape(640, 128)
            column = (ty * 3 + tx) * 128
            taps[pair, :, column:column + 128] = part.astype(BF16)


def tap_of(w_ref, tap):
    value = w_ref[tap].astype(F32)
    return jnp.concatenate([value, value], axis=1)


def widen(w_ref, wide, backward):
    low = lax.broadcasted_iota(jnp.int32, (1, 128), 1) < 64
    for tz in range(3):
        for q in range(9):
            tap = tz * 9 + q
            value = tap_of(w_ref, 26 - tap if backward else tap)
            a, b = (q, tz) if backward else (tz, q)
            lanes = pl.ds(b * 128, 128)
            wide[pl.ds(a * 128, 64), lanes] = jnp.where(low, value, 0.0).astype(BF16)
            wide[pl.ds(a * 128 + 64, 64), lanes] = jnp.where(low, 0.0, value).astype(BF16)


def convolve(taps, wide, backward=False):
    contract = (((1,), (0 if backward else 1,)), ((), ()))
    wide = lax.dot_general(taps, wide[...], contract, preferred_element_type=F32)
    return wide[0:512, 0:128] + wide[64:576, 128:256] + wide[128:640, 256:384]


def spread(wide_g, pair, value):
    for tz in range(3):
        wide_g[pair, tz * 64:tz * 64 + 512, tz * 128:tz * 128 + 128] = value


def outer(one, other):
    return lax.dot_general(
        one[...].reshape(PAIRS * 640, one.shape[2]),
        other[...].reshape(PAIRS * 640, other.shape[2]),
        (((0,), (0,)), ((), ())),
        preferred_element_type=F32,
    )


def block_kernel(cap, count_ref, list_ref, pos_ref, par_ref, f_ref, c_ref, w_ref, v_ref,
                 o_out, grads_out,
                 rows_x, rows_g, rows_h, line_x, line_g, line_h, src_x, src_g, src_h, xs, gs, hs, scratch, cube, taps,
                 taps_g, wide_g, wide_w, wide_b, wide_v, product, product_g, p_sum,
                 r1, a1, r2, r4, whole, send, recv, send_sum, recv_sum):
    g, y, x, c = place()
    sibling = device(g, y, x, 1 - c)
    layer = [
        ((y + ky) % N_Y, (x + kx) % N_X, ky * N_X + kx)
        for ky in range(N_Y)
        for kx in range(N_X)
        if (ky, kx) != (0, 0)
    ]
    layer.sort(key=lambda to: -sum(min(k, 4 - k) for k in divmod(to[2], N_X)))
    zs = [device((g + k) % N_Z, y, x, c) for k in (4, 3, 5, 2, 6, 1, 7)]
    partners = [sibling] + [device(g, yy, xx, c) for yy, xx, _ in layer] + zs
    partners += [device((g + k) % N_Z, y, x, 1 - c) for k in (1, N_Z - 1)]
    barrier = pltpu.get_barrier_semaphore()
    for partner in partners:
        pl.semaphore_signal(barrier, inc=1, device_id=partner, device_id_type=MESH)

    count = count_ref[g, lax.axis_index("dev")]
    low = lax.broadcasted_iota(jnp.int32, (1, 128), 1) < 64
    started = []
    gx = Gather(0, cap, list_ref, rows_x, line_x, src_x, send, recv, started)
    gg = Gather(1, cap, list_ref, rows_g, line_g, src_g, send, recv, started)
    gh = Gather(2, cap, list_ref, rows_h, line_h, src_h, send, recv, started)

    def live(pair):
        return jnp.where(low, 2 * pair, 2 * pair + 1) < count

    def over_pairs(body):
        def step(pair, carry):
            body(pair)
            return carry

        lax.fori_loop(0, PAIRS, step, 0)

    def pack_x(pair):
        value = f_ref[pair].astype(F32).T
        xs[pair] = value.astype(BF16)
        gx.write(pair, value, scratch)

    def pack_g(pair):
        value = jnp.where(live(pair), c_ref[pair].astype(F32).T, 0.0)
        gs[pair] = value.astype(BF16)
        gg.write(pair, value, scratch)

    def forward(pair):
        build_cube(cube, xs[pair].astype(F32), rows_x, pos_ref, par_ref, pair)
        stack_taps(cube, taps, pair)
        first = convolve(taps[pair], wide_w)
        hidden = jnp.where(live(pair), jnp.maximum(first, 0.0), 0.0)
        hidden = hidden.astype(BF16).astype(F32)
        hs[pair] = hidden.astype(BF16)
        gh.write(pair, hidden, scratch)

    def backward(pair):
        build_cube(cube, gs[pair].astype(F32), rows_g, pos_ref, par_ref, pair)
        stack_taps(cube, taps_g, pair)
        back = convolve(taps_g[pair], wide_b, True)
        grad = jnp.where(hs[pair].astype(F32) > 0, back, 0.0)
        spread(wide_g, pair, grad.astype(BF16))

    def finish(pair):
        build_cube(cube, hs[pair].astype(F32), rows_h, pos_ref, par_ref, pair)
        stack_taps(cube, taps, pair)
        second = convolve(taps[pair], wide_v)
        lane = lax.broadcasted_iota(jnp.int32, (128, 1), 0)
        slot = jnp.where(lane < 64, 2 * pair, 2 * pair + 1)
        result = f_ref[pair].astype(F32) + second.T
        o_out[pair] = jnp.where(slot < count, result, 0.0).astype(BF16)

    over_pairs(pack_x)
    pl.semaphore_wait(barrier, len(partners))
    gx.begin()
    for one in (gx, gg, gh):
        one.clear()
    gx.step0()
    over_pairs(pack_g)
    gx.step1()
    gg.begin()
    widen(w_ref, wide_w, False)
    gx.step2()
    gg.step0()
    widen(v_ref, wide_b, True)
    gx.step3()
    gg.step1()
    widen(v_ref, wide_v, False)
    wide_g[...] = jnp.zeros((PAIRS, 640, 384), BF16)
    gx.step4()
    gx.step5()
    gg.step2()
    gx.step6()
    over_pairs(forward)
    gh.begin()
    gg.step3()
    gh.step0()
    gh.step1()
    gg.step4()
    gg.step5()
    gh.step2()
    gg.step6()
    over_pairs(backward)
    gh.step3()
    product[...] = outer(wide_g, taps)
    gh.step4()
    for q in range(9):
        for tz in range(3):
            even, odd = pl.ds(tz * 128, 64), pl.ds(tz * 128 + 64, 64)
            lanes = pl.ds(q * 128, 128)
            one = product[even, lanes] + pltpu.roll(product[odd, lanes], 64, 1)
            p_sum[pl.ds((q * 3 + tz) * 64, 64), :] = one
    p_sum[1728:2048, :] = jnp.zeros((320, 128), F32)
    over_pairs(lambda pair: spread(wide_g, pair, hs[pair]))
    product_g[...] = outer(taps_g, wide_g)
    for q in range(9):
        for tz in range(3):
            even, odd = pl.ds((8 - q) * 128, 64), pl.ds((8 - q) * 128 + 64, 64)
            lanes = pl.ds((2 - tz) * 128, 128)
            rows = pl.ds((q * 3 + tz) * 64, 64)
            two = pltpu.roll(product_g[even, lanes], 64, 1) + product_g[odd, lanes]
            p_sum[rows, :] = jnp.where(low, p_sum[rows, :], two)

    used = [0]

    def copy(src, dst, target):
        number = used[0]
        used[0] += 1
        one = pltpu.make_async_remote_copy(
            src_ref=src, dst_ref=dst, send_sem=send_sum.at[number],
            recv_sem=recv_sum.at[number], device_id=target, device_id_type=MESH,
        )
        one.start()
        return one

    one = copy(p_sum.at[pl.ds((1 - c) * 1024, 1024)], r1, sibling)
    gh.step5()
    one.wait()
    a1[...] = (p_sum[pl.ds(c * 1024, 1024)] + r1[...]).astype(BF16)

    made = [
        copy(a1.at[pl.ds((yy * N_X + xx) * 64, 64)], r2.at[k], device(g, yy, xx, c))
        for yy, xx, k in layer
    ]
    gh.step6()
    finish(0)
    for one in made:
        one.wait()
    at = y * N_X + x
    part = a1[pl.ds(at * 64, 64)].astype(F32)
    for k in range(1, 16):
        part = part + r2[k].astype(F32)
    r4[g] = part.astype(BF16)

    made = [copy(r4.at[g], r4.at[g], target) for target in zs]
    finish(1)
    for one in made:
        one.wait()
    part = r4[0].astype(F32)
    for k in range(1, N_Z):
        part = part + r4[k].astype(F32)
    rows = pl.ds(c * 1024 + at * 64, 64)
    whole[rows] = part.astype(BF16)

    made = [
        copy(whole.at[rows], whole.at[rows], device(g, yy, xx, c)) for yy, xx, _ in layer
    ]
    passed = [copy(whole.at[rows], whole.at[rows], sibling)]
    finish(2)
    for one, (_, _, k) in zip(made, layer):
        one.wait()
        ky, kx = divmod(k, N_X)
        origin = (y - ky + N_Y) % N_Y * N_X + (x - kx + N_X) % N_X
        part = whole.at[pl.ds(c * 1024 + origin * 64, 64)]
        passed.append(copy(part, part, sibling))
    for one in passed:
        one.wait()
    for q in range(9):
        for tz in range(3):
            grads_out[tz * 9 + q] = whole[pl.ds((q * 3 + tz) * 64, 64)]
    for one in started:
        one.wait_send()


def block(cap, collective_id, counts, lists, pos, parity, features, cotangent, w, v):
    smem, vmem = pl.BlockSpec(memory_space=pltpu.SMEM), pl.BlockSpec(memory_space=pltpu.VMEM)
    return pl.pallas_call(
        functools.partial(block_kernel, cap),
        in_specs=[smem] * 4 + [vmem] * 4,
        out_specs=[vmem] * 2,
        out_shape=[
            jax.ShapeDtypeStruct((PAIRS, 128, 512), BF16),
            jax.ShapeDtypeStruct((27, 64, 128), BF16),
        ],
        scratch_shapes=[pltpu.VMEM((2, 97, 3, 64, 128), BF16)] * 3
        + [pltpu.VMEM((24, 3, 64, 128), BF16)] * 3
        + [pltpu.VMEM((2, PAIRS, 3, 64, 128), BF16)] * 3
        + [pltpu.VMEM((PAIRS, 512, 128), BF16)] * 3
        + [
            pltpu.VMEM((512, 128), F32),
            pltpu.VMEM((10, 10, 24, 128), F32),
            pltpu.VMEM((PAIRS, 640, 1152), BF16),
            pltpu.VMEM((PAIRS, 640, 1152), BF16),
            pltpu.VMEM((PAIRS, 640, 384), BF16),
            pltpu.VMEM((384, 1152), BF16),
            pltpu.VMEM((1152, 384), BF16),
            pltpu.VMEM((384, 1152), BF16),
            pltpu.VMEM((384, 1152), F32),
            pltpu.VMEM((1152, 384), F32),
            pltpu.VMEM((2048, 128), F32),
            pltpu.VMEM((1024, 128), F32),
            pltpu.VMEM((1024, 128), BF16),
            pltpu.VMEM((16, 64, 128), BF16),
            pltpu.VMEM((N_Z, 64, 128), BF16),
            pltpu.VMEM((2048, 128), BF16),
            pltpu.SemaphoreType.DMA((3, 20)),
            pltpu.SemaphoreType.DMA((3, 20)),
            pltpu.SemaphoreType.DMA((56,)),
            pltpu.SemaphoreType.DMA((56,)),
        ],
        compiler_params=pltpu.CompilerParams(
            collective_id=collective_id, has_side_effects=True, vmem_limit_bytes=62 * 2**20
        ),
    )(counts, lists, pos, parity, features, cotangent, w, v)


def table_kernel(counts_ref, near_ref, needed_out, list_out, pos_out, par_out):
    g, y, x, c = place()
    iota = lambda shape, dim: lax.broadcasted_iota(jnp.int32, shape, dim)
    rows = (lambda d: d >> 3, lambda d: (d >> 1) & 3)
    orders = (lambda d: (d >> 1 & 3) * 2 + (d & 1), lambda d: (d >> 3) * 2 + (d & 1))
    pairs = ((counts_ref[...] + 1) >> 1).astype(F32)
    other, this = iota((32, 32), 0), iota((32, 32), 1)
    base = []
    for half in range(2):
        before = (rows[half](other) == rows[half](this)) & (
            orders[half](other) < orders[half](this)
        )
        base.append(jnp.dot(pairs, before.astype(F32), preferred_element_type=F32))
    top = jnp.max(jnp.maximum(base[0], base[1]) + pairs)
    needed_out[0] = top.astype(jnp.int32)

    group = iota((N_Z, 32), 0)

    def of_group(value, which):
        return jnp.sum(jnp.where(group == which, value, 0.0), axis=0, keepdims=True)

    near = near_ref[...]
    owner = (near * 10923) >> 16
    within = near - 6 * owner
    dev = owner & 31
    lane, device_lane = iota((6, 26), 1), iota((6, 32), 1)
    pos = jnp.zeros((6, 26), jnp.int32)
    for k, direction in enumerate(DIRECTIONS):
        half = face_of(direction)[0]
        line = of_group(base[half], g + direction[0])
        hit = dev[:, k:k + 1] == device_lane
        rank = jnp.sum(jnp.where(hit, line, 0.0), axis=1, keepdims=True).astype(jnp.int32)
        pos = jnp.where(lane == k, rank + rows[half](dev) * 24, pos)
    pos_out[...] = jnp.where(near >= 0, pos + (within >> 1), 96)
    par_out[...] = within & 1

    lead = c == 0
    d = iota((24, 32), 1)
    own_row = jnp.where(lead, y, x)
    inside = jnp.where(lead, rows[0](d), rows[1](d)) == own_row
    order = jnp.where(lead, orders[0](d), orders[1](d))
    start = jnp.where(lead, base[0], base[1])
    for source, which in enumerate((g, (g + jnp.where(lead, 1, N_Z - 1)) % N_Z)):
        rank = of_group(start, which).astype(jnp.int32)
        size = of_group(pairs, which).astype(jnp.int32)
        found = jnp.zeros((24, 1), F32)
        for p in range(3):
            match = inside & (rank + p == iota((24, 32), 0)) & (size > p)
            found += jnp.sum(
                jnp.where(match, (order * 3 + p).astype(F32), 0.0), axis=1, keepdims=True
            )
        list_out[:, source:source + 1] = found.astype(jnp.int32)


def tables(counts, neighbours):
    vmem = pl.BlockSpec(memory_space=pltpu.VMEM)
    return pl.pallas_call(
        table_kernel,
        in_specs=[vmem] * 2,
        out_specs=[pl.BlockSpec(memory_space=pltpu.SMEM)] + [vmem] * 3,
        out_shape=[
            jax.ShapeDtypeStruct((1,), jnp.int32),
            jax.ShapeDtypeStruct((24, 2), jnp.int32),
            jax.ShapeDtypeStruct((6, 26), jnp.int32),
            jax.ShapeDtypeStruct((6, 26), jnp.int32),
        ],
    )(counts, neighbours)


def per_device(features, cotangent, first_weight, second_weight, counts, neighbours):
    needed, lists, pos, parity = tables(counts, neighbours)
    operands = (
        counts,
        lists,
        pos,
        parity,
        features.reshape(PAIRS, 128, 512),
        cotangent.reshape(PAIRS, 128, 512),
        first_weight.transpose(1, 0, 2),
        second_weight.transpose(1, 0, 2),
    )
    out, grads = lax.switch(
        sum((needed[0] > cap).astype(jnp.int32) for cap in CAPS[:-1]),
        [functools.partial(block, cap, i) for i, cap in enumerate(CAPS)],
        *operands,
    )
    return (
        out.reshape(6, 64, 512),
        grads[:, :, :64].astype(F32).transpose(1, 0, 2),
        grads[:, :, 64:].astype(F32).transpose(1, 0, 2),
    )


def solution(mesh):
    placed = (
        P(("group", "dev"), None, None),
        P(("group", "dev"), None, None),
        P(),
        P(),
        P(),
        P(("group", "dev"), None),
    )
    return jax.shard_map(
        per_device,
        mesh=mesh,
        in_specs=placed,
        out_specs=(P(("group", "dev"), None, None), P(), P()),
        check_vma=False,
    )
```

```python
import functools

import jax
import jax.numpy as jnp
import numpy as np
from jax import lax
from jax.experimental import pallas as pl
from jax.experimental.pallas import tpu as pltpu
from jax.sharding import PartitionSpec as P

MESH = pl.DeviceIdType.MESH
F32 = jnp.float32
BF16 = jnp.bfloat16
N_Z, N_Y, N_X = 8, 4, 4
PAIRS = 3
CAPS = (14, 16, 24)
DIRECTIONS = [
    (dz, dy, dx)
    for dz in (-1, 0, 1)
    for dy in (-1, 0, 1)
    for dx in (-1, 0, 1)
    if (dz, dy, dx) != (0, 0, 0)
]


def face_of(direction):
    dz, dy, dx = direction
    if dz != 0:
        return (0 if dz == 1 else 1), 2
    if dx != 0:
        return (0 if dx == 1 else 1), 0
    return (0 if dy == 1 else 1), 1


def place():
    d = lax.axis_index("dev")
    return lax.axis_index("group"), d // 8, (d // 2) % 4, d % 2


def device(g, y, x, c):
    return (g, (y * 4 + x) * 2 + c)


class Gather:
    def __init__(self, field, cap, list_ref, rows, line, src, send, recv, started):
        self.field, self.cap, self.list_ref = field, cap, list_ref
        self.rows, self.line, self.src = rows, line, src
        self.send, self.recv, self.started = send, recv, started
        self.g, self.y, self.x, self.c = place()
        self.i = self.first(self.c)
        self.j = self.first(1 - self.c)
        self.made = dict()

    def first(self, half):
        return self.x * (1 - half) + self.y * half

    def moved(self, first, step):
        along_y = self.c if first else 1 - self.c
        y = (self.y + step * along_y + N_Y) % N_Y
        x = (self.x + step * (1 - along_y) + N_X) % N_X
        return device(self.g, y, x, self.c)

    def row(self, step):
        return pl.ds((self.j + step + 4) % 4 * 24, self.cap)

    def block(self, step):
        return pl.ds((self.i + step + 4) % 4 * 6, 6)

    def sibling(self):
        return device(self.g, self.y, self.x, 1 - self.c)

    def describe(self, number, came, src, dst, target):
        return pltpu.make_async_remote_copy(
            src_ref=src,
            dst_ref=dst,
            send_sem=self.send.at[self.field, number],
            recv_sem=self.recv.at[self.field, came],
            device_id=target,
            device_id_type=MESH,
        )

    def copy(self, number, came, src, dst, target):
        one = self.describe(number, came, src, dst, target)
        one.start()
        self.started.append(one)
        self.made[number] = one

    def same(self, number, part, target):
        self.copy(number, number, part, part, target)

    def came(self, *numbers):
        for number in numbers:
            self.made[number].wait_recv()

    def write(self, pair, value, scratch):
        scratch[...] = value
        cube = value.reshape(8, 8, 8, 128)
        for half, edge in ((0, 0), (1, 7)):
            self.src[half, pair, 0] = scratch[pl.ds(edge, 64, stride=8), :].astype(BF16)
            self.src[half, pair, 1] = cube[:, edge].reshape(64, 128).astype(BF16)
            self.src[half, pair, 2] = value[edge * 64:edge * 64 + 64].astype(BF16)

    def clear(self):
        for half in range(2):
            self.rows[half, 96:97] = jnp.zeros((1, 3, 64, 128), BF16)

    def begin(self):
        sides, plane, c = pl.ds(0, 2), pl.ds(2, 1), self.c
        for half, step in ((0, N_Z - 1), (1, 1)):
            target = device((self.g + step) % N_Z, self.y, self.x, half)
            dst = self.line.at[pl.ds(self.first(half) * 6 + c * 3, 3), plane]
            self.copy(1 + half, 1 + c, self.src.at[half, :, plane], dst, target)
        dst = self.line.at[pl.ds(self.first(1 - c) * 6 + c * 3, 3), sides]
        self.copy(0, 0, self.src.at[1 - c, :, sides], dst, self.sibling())
        self.line[pl.ds(self.i * 6 + c * 3, 3), 0:2] = self.src[c, :, 0:2]

    def both_ways(self, number, part, first):
        lower, upper = (part + (slice(None), pl.ds(start, 32)) for start in (0, 32))
        ref = self.line if first else self.rows
        ahead, back = self.moved(first, 1), self.moved(first, -1)
        self.same(number, ref.at[lower], ahead)
        self.same(number + 1, ref.at[upper], back)
        self.same(number + 2, ref.at[upper], ahead)
        self.same(number + 3, ref.at[lower], back)

    def step0(self):
        self.came(0)
        part = self.line.at[pl.ds(0, 3), pl.ds(2, 1)]
        for core in range(2):
            self.describe(1, 1 + core, part, part, self.sibling()).wait_recv()
        self.both_ways(3, (self.block(0),), True)

    def step1(self):
        for number, step, start in ((7, 1, 0), (8, -1, 32)):
            self.came(number - 4)
            part = self.line.at[self.block(-step), :, pl.ds(start, 32)]
            self.same(number, part, self.moved(True, step))

    def step2(self):
        self.came(5, 6, 7, 8)

        def one(k, carry):
            at = self.j * 24 + k
            self.rows[self.c, at, 0:2] = self.line[self.list_ref[k, 0], 0:2]
            self.rows[self.c, at, 2:3] = self.line[self.list_ref[k, 1], 2:3]
            return carry

        lax.fori_loop(0, self.cap, one, 0)
        self.both_ways(9, (self.c, self.row(0)), False)
        self.same(15, self.rows.at[self.c, self.row(0)], self.sibling())

    def step3(self):
        for number, step, start in ((13, 1, 0), (14, -1, 32)):
            self.came(number - 4)
            part = self.rows.at[self.c, self.row(-step), :, pl.ds(start, 32)]
            self.same(number, part, self.moved(False, step))

    def step4(self):
        for number, step in ((16, 1), (17, -1)):
            self.came(number - 5)
            self.same(number, self.rows.at[self.c, self.row(-step)], self.sibling())

    def step5(self):
        for number, start in ((13, 0), (14, 32)):
            self.came(number)
            part = self.rows.at[self.c, self.row(2), :, pl.ds(start, 32)]
            self.same(number + 5, part, self.sibling())

    def step6(self):
        self.came(15, 16, 17, 18, 19)


def build_cube(cube, own, rows_ref, pos_ref, par_ref, pair):
    low = lax.broadcasted_iota(jnp.int32, (1, 128), 1) < 64
    cube[1:9, 1:9, 8:16, :] = own.reshape(8, 8, 8, 128)
    for k, (dz, dy, dx) in enumerate(DIRECTIONS):
        half, face = face_of((dz, dy, dx))
        if dz != 0 and dy != 0:
            start, count = (0, 16) if dy == 1 else (48, 16)
        else:
            start, count = 0, 64
        picked = []
        for s in range(2):
            at = pos_ref[2 * pair + s, k]
            value = rows_ref[half, at, face, start:start + count].astype(F32)
            turned = pltpu.roll(value, 64, 1)
            picked.append(jnp.where(par_ref[2 * pair + s, k] == s, value, turned))
        piece = jnp.where(low, picked[0], picked[1])
        if count == 16:
            piece = piece[0:8] if dy == 1 else piece[8:16]
        zz = {-1: 0, 1: 9}.get(dz)
        yy = {-1: 0, 1: 9}.get(dy)
        if dx == 0:
            if dz == 0:
                cube[1:9, yy, 8:16, :] = piece.reshape(8, 8, 128)
            elif dy == 0:
                cube[zz, 1:9, 8:16, :] = piece.reshape(8, 8, 128)
            else:
                cube[zz, yy, 8:16, :] = piece
            continue
        sub = 7 if dx == -1 else 16
        edge_x = 7 if dx == -1 else 0
        edge_y = 7 if dy == -1 else 0
        if dz == 0 and dy == 0:
            rows = [(z + 1, q + 1, z * 8 + q) for z in range(8) for q in range(8)]
        elif dz == 0:
            rows = [(z + 1, yy, z * 8 + edge_y) for z in range(8)]
        elif dy == 0:
            rows = [(zz, q + 1, q * 8 + edge_x) for q in range(8)]
        else:
            rows = [(zz, yy, edge_x)]
        for a, b, r in rows:
            cube[a, b, sub:sub + 1, :] = piece[r:r + 1]


def stack_taps(cube, taps, pair):
    for ty in range(3):
        for tx in range(3):
            part = cube[:, ty:ty + 8, 7 + tx:15 + tx, :].reshape(640, 128)
            column = (ty * 3 + tx) * 128
            taps[pair, :, column:column + 128] = part.astype(BF16)


def tap_of(w_ref, tap):
    value = w_ref[tap].astype(F32)
    return jnp.concatenate([value, value], axis=1)


def widen(w_ref, wide, backward):
    low = lax.broadcasted_iota(jnp.int32, (1, 128), 1) < 64
    for tz in range(3):
        for q in range(9):
            tap = tz * 9 + q
            value = tap_of(w_ref, 26 - tap if backward else tap)
            a, b = (q, tz) if backward else (tz, q)
            lanes = pl.ds(b * 128, 128)
            wide[pl.ds(a * 128, 64), lanes] = jnp.where(low, value, 0.0).astype(BF16)
            wide[pl.ds(a * 128 + 64, 64), lanes] = jnp.where(low, 0.0, value).astype(BF16)


def convolve(taps, wide, backward=False):
    contract = (((1,), (0 if backward else 1,)), ((), ()))
    wide = lax.dot_general(taps, wide[...], contract, preferred_element_type=F32)
    return wide[0:512, 0:128] + wide[64:576, 128:256] + wide[128:640, 256:384]


def spread(wide_g, pair, value):
    for tz in range(3):
        wide_g[pair, tz * 64:tz * 64 + 512, tz * 128:tz * 128 + 128] = value


def outer(one, other):
    return lax.dot_general(
        one[...].reshape(PAIRS * 640, one.shape[2]),
        other[...].reshape(PAIRS * 640, other.shape[2]),
        (((0,), (0,)), ((), ())),
        preferred_element_type=F32,
    )


def block_kernel(cap, count_ref, list_ref, pos_ref, par_ref, f_ref, c_ref, w_ref, v_ref,
                 o_out, grads_out,
                 rows_x, rows_g, rows_h, line_x, line_g, line_h, src_x, src_g, src_h, xs, gs, hs, scratch, cube, taps,
                 taps_g, wide_g, wide_w, wide_b, wide_v, product, product_g, p_sum,
                 r1, a1, r2, r4, whole, send, recv, send_sum, recv_sum):
    g, y, x, c = place()
    sibling = device(g, y, x, 1 - c)
    layer = [
        ((y + ky) % N_Y, (x + kx) % N_X, ky * N_X + kx)
        for ky in range(N_Y)
        for kx in range(N_X)
        if (ky, kx) != (0, 0)
    ]
    layer.sort(key=lambda to: -sum(min(k, 4 - k) for k in divmod(to[2], N_X)))
    zs = [device((g + k) % N_Z, y, x, c) for k in (4, 3, 5, 2, 6, 1, 7)]
    partners = [sibling] + [device(g, yy, xx, c) for yy, xx, _ in layer] + zs
    partners += [device((g + k) % N_Z, y, x, 1 - c) for k in (1, N_Z - 1)]
    barrier = pltpu.get_barrier_semaphore()
    for partner in partners:
        pl.semaphore_signal(barrier, inc=1, device_id=partner, device_id_type=MESH)

    count = count_ref[g, lax.axis_index("dev")]
    low = lax.broadcasted_iota(jnp.int32, (1, 128), 1) < 64
    started = []
    gx = Gather(0, cap, list_ref, rows_x, line_x, src_x, send, recv, started)
    gg = Gather(1, cap, list_ref, rows_g, line_g, src_g, send, recv, started)
    gh = Gather(2, cap, list_ref, rows_h, line_h, src_h, send, recv, started)

    def live(pair):
        return jnp.where(low, 2 * pair, 2 * pair + 1) < count

    def over_pairs(body):
        def step(pair, carry):
            body(pair)
            return carry

        lax.fori_loop(0, PAIRS, step, 0)

    def pack_x(pair):
        value = f_ref[pair].astype(F32).T
        xs[pair] = value.astype(BF16)
        gx.write(pair, value, scratch)

    def pack_g(pair):
        value = jnp.where(live(pair), c_ref[pair].astype(F32).T, 0.0)
        gs[pair] = value.astype(BF16)
        gg.write(pair, value, scratch)

    def forward(pair):
        build_cube(cube, xs[pair].astype(F32), rows_x, pos_ref, par_ref, pair)
        stack_taps(cube, taps, pair)
        first = convolve(taps[pair], wide_w)
        hidden = jnp.where(live(pair), jnp.maximum(first, 0.0), 0.0)
        hidden = hidden.astype(BF16).astype(F32)
        hs[pair] = hidden.astype(BF16)
        gh.write(pair, hidden, scratch)

    def backward(pair):
        build_cube(cube, gs[pair].astype(F32), rows_g, pos_ref, par_ref, pair)
        stack_taps(cube, taps_g, pair)
        back = convolve(taps_g[pair], wide_b, True)
        grad = jnp.where(hs[pair].astype(F32) > 0, back, 0.0)
        spread(wide_g, pair, grad.astype(BF16))

    def finish(pair):
        build_cube(cube, hs[pair].astype(F32), rows_h, pos_ref, par_ref, pair)
        stack_taps(cube, taps, pair)
        second = convolve(taps[pair], wide_v)
        lane = lax.broadcasted_iota(jnp.int32, (128, 1), 0)
        slot = jnp.where(lane < 64, 2 * pair, 2 * pair + 1)
        result = f_ref[pair].astype(F32) + second.T
        o_out[pair] = jnp.where(slot < count, result, 0.0).astype(BF16)

    over_pairs(pack_x)
    pl.semaphore_wait(barrier, len(partners))
    gx.begin()
    for one in (gx, gg, gh):
        one.clear()
    gx.step0()
    over_pairs(pack_g)
    gx.step1()
    gg.begin()
    widen(w_ref, wide_w, False)
    gx.step2()
    gg.step0()
    widen(v_ref, wide_b, True)
    gx.step3()
    gg.step1()
    widen(v_ref, wide_v, False)
    wide_g[...] = jnp.zeros((PAIRS, 640, 384), BF16)
    gx.step4()
    gx.step5()
    gg.step2()
    gx.step6()
    over_pairs(forward)
    gh.begin()
    gg.step3()
    gh.step0()
    gh.step1()
    gg.step4()
    gh.step2()
    gg.step5()
    gg.step6()
    over_pairs(backward)
    gh.step3()
    product[...] = outer(wide_g, taps)
    gh.step4()
    for q in range(9):
        for tz in range(3):
            even, odd = pl.ds(tz * 128, 64), pl.ds(tz * 128 + 64, 64)
            lanes = pl.ds(q * 128, 128)
            one = product[even, lanes] + pltpu.roll(product[odd, lanes], 64, 1)
            p_sum[pl.ds((q * 3 + tz) * 64, 64), :] = one
    p_sum[1728:2048, :] = jnp.zeros((320, 128), F32)
    over_pairs(lambda pair: spread(wide_g, pair, hs[pair]))
    product_g[...] = outer(taps_g, wide_g)
    for q in range(9):
        for tz in range(3):
            even, odd = pl.ds((8 - q) * 128, 64), pl.ds((8 - q) * 128 + 64, 64)
            lanes = pl.ds((2 - tz) * 128, 128)
            rows = pl.ds((q * 3 + tz) * 64, 64)
            two = pltpu.roll(product_g[even, lanes], 64, 1) + product_g[odd, lanes]
            p_sum[rows, :] = jnp.where(low, p_sum[rows, :], two)

    used = [0]

    def copy(src, dst, target):
        number = used[0]
        used[0] += 1
        one = pltpu.make_async_remote_copy(
            src_ref=src, dst_ref=dst, send_sem=send_sum.at[number],
            recv_sem=recv_sum.at[number], device_id=target, device_id_type=MESH,
        )
        one.start()
        return one

    one = copy(p_sum.at[pl.ds((1 - c) * 1024, 1024)], r1, sibling)
    gh.step5()
    one.wait()
    a1[...] = (p_sum[pl.ds(c * 1024, 1024)] + r1[...]).astype(BF16)

    made = [
        copy(a1.at[pl.ds((yy * N_X + xx) * 64, 64)], r2.at[k], device(g, yy, xx, c))
        for yy, xx, k in layer
    ]
    gh.step6()
    finish(0)
    for one in made:
        one.wait()
    at = y * N_X + x
    part = a1[pl.ds(at * 64, 64)].astype(F32)
    for k in range(1, 16):
        part = part + r2[k].astype(F32)
    r4[g] = part.astype(BF16)

    made = [copy(r4.at[g], r4.at[g], target) for target in zs]
    finish(1)
    for one in made:
        one.wait()
    part = r4[0].astype(F32)
    for k in range(1, N_Z):
        part = part + r4[k].astype(F32)
    rows = pl.ds(c * 1024 + at * 64, 64)
    whole[rows] = part.astype(BF16)

    made = [
        copy(whole.at[rows], whole.at[rows], device(g, yy, xx, c)) for yy, xx, _ in layer
    ]
    passed = [copy(whole.at[rows], whole.at[rows], sibling)]
    finish(2)
    for one, (_, _, k) in zip(made, layer):
        one.wait()
        ky, kx = divmod(k, N_X)
        origin = (y - ky + N_Y) % N_Y * N_X + (x - kx + N_X) % N_X
        part = whole.at[pl.ds(c * 1024 + origin * 64, 64)]
        passed.append(copy(part, part, sibling))
    for one in passed:
        one.wait()
    for q in range(9):
        for tz in range(3):
            grads_out[tz * 9 + q] = whole[pl.ds((q * 3 + tz) * 64, 64)]
    for one in started:
        one.wait_send()


def block(cap, collective_id, counts, lists, pos, parity, features, cotangent, w, v):
    smem, vmem = pl.BlockSpec(memory_space=pltpu.SMEM), pl.BlockSpec(memory_space=pltpu.VMEM)
    return pl.pallas_call(
        functools.partial(block_kernel, cap),
        in_specs=[smem] * 4 + [vmem] * 4,
        out_specs=[vmem] * 2,
        out_shape=[
            jax.ShapeDtypeStruct((PAIRS, 128, 512), BF16),
            jax.ShapeDtypeStruct((27, 64, 128), BF16),
        ],
        scratch_shapes=[pltpu.VMEM((2, 97, 3, 64, 128), BF16)] * 3
        + [pltpu.VMEM((24, 3, 64, 128), BF16)] * 3
        + [pltpu.VMEM((2, PAIRS, 3, 64, 128), BF16)] * 3
        + [pltpu.VMEM((PAIRS, 512, 128), BF16)] * 3
        + [
            pltpu.VMEM((512, 128), F32),
            pltpu.VMEM((10, 10, 24, 128), F32),
            pltpu.VMEM((PAIRS, 640, 1152), BF16),
            pltpu.VMEM((PAIRS, 640, 1152), BF16),
            pltpu.VMEM((PAIRS, 640, 384), BF16),
            pltpu.VMEM((384, 1152), BF16),
            pltpu.VMEM((1152, 384), BF16),
            pltpu.VMEM((384, 1152), BF16),
            pltpu.VMEM((384, 1152), F32),
            pltpu.VMEM((1152, 384), F32),
            pltpu.VMEM((2048, 128), F32),
            pltpu.VMEM((1024, 128), F32),
            pltpu.VMEM((1024, 128), BF16),
            pltpu.VMEM((16, 64, 128), BF16),
            pltpu.VMEM((N_Z, 64, 128), BF16),
            pltpu.VMEM((2048, 128), BF16),
            pltpu.SemaphoreType.DMA((3, 20)),
            pltpu.SemaphoreType.DMA((3, 20)),
            pltpu.SemaphoreType.DMA((56,)),
            pltpu.SemaphoreType.DMA((56,)),
        ],
        compiler_params=pltpu.CompilerParams(
            collective_id=collective_id, has_side_effects=True, vmem_limit_bytes=62 * 2**20
        ),
    )(counts, lists, pos, parity, features, cotangent, w, v)


def table_kernel(counts_ref, near_ref, needed_out, list_out, pos_out, par_out):
    g, y, x, c = place()
    iota = lambda shape, dim: lax.broadcasted_iota(jnp.int32, shape, dim)
    rows = (lambda d: d >> 3, lambda d: (d >> 1) & 3)
    orders = (lambda d: (d >> 1 & 3) * 2 + (d & 1), lambda d: (d >> 3) * 2 + (d & 1))
    pairs = ((counts_ref[...] + 1) >> 1).astype(F32)
    other, this = iota((32, 32), 0), iota((32, 32), 1)
    base = []
    for half in range(2):
        before = (rows[half](other) == rows[half](this)) & (
            orders[half](other) < orders[half](this)
        )
        base.append(jnp.dot(pairs, before.astype(F32), preferred_element_type=F32))
    top = jnp.max(jnp.maximum(base[0], base[1]) + pairs)
    needed_out[0] = top.astype(jnp.int32)

    group = iota((N_Z, 32), 0)

    def of_group(value, which):
        return jnp.sum(jnp.where(group == which, value, 0.0), axis=0, keepdims=True)

    near = near_ref[...]
    owner = (near * 10923) >> 16
    within = near - 6 * owner
    dev = owner & 31
    lane, device_lane = iota((6, 26), 1), iota((6, 32), 1)
    pos = jnp.zeros((6, 26), jnp.int32)
    for k, direction in enumerate(DIRECTIONS):
        half = face_of(direction)[0]
        line = of_group(base[half], g + direction[0])
        hit = dev[:, k:k + 1] == device_lane
        rank = jnp.sum(jnp.where(hit, line, 0.0), axis=1, keepdims=True).astype(jnp.int32)
        pos = jnp.where(lane == k, rank + rows[half](dev) * 24, pos)
    pos_out[...] = jnp.where(near >= 0, pos + (within >> 1), 96)
    par_out[...] = within & 1

    lead = c == 0
    d = iota((24, 32), 1)
    own_row = jnp.where(lead, y, x)
    inside = jnp.where(lead, rows[0](d), rows[1](d)) == own_row
    order = jnp.where(lead, orders[0](d), orders[1](d))
    start = jnp.where(lead, base[0], base[1])
    for source, which in enumerate((g, (g + jnp.where(lead, 1, N_Z - 1)) % N_Z)):
        rank = of_group(start, which).astype(jnp.int32)
        size = of_group(pairs, which).astype(jnp.int32)
        found = jnp.zeros((24, 1), F32)
        for p in range(3):
            match = inside & (rank + p == iota((24, 32), 0)) & (size > p)
            found += jnp.sum(
                jnp.where(match, (order * 3 + p).astype(F32), 0.0), axis=1, keepdims=True
            )
        list_out[:, source:source + 1] = found.astype(jnp.int32)


def tables(counts, neighbours):
    vmem = pl.BlockSpec(memory_space=pltpu.VMEM)
    return pl.pallas_call(
        table_kernel,
        in_specs=[vmem] * 2,
        out_specs=[pl.BlockSpec(memory_space=pltpu.SMEM)] + [vmem] * 3,
        out_shape=[
            jax.ShapeDtypeStruct((1,), jnp.int32),
            jax.ShapeDtypeStruct((24, 2), jnp.int32),
            jax.ShapeDtypeStruct((6, 26), jnp.int32),
            jax.ShapeDtypeStruct((6, 26), jnp.int32),
        ],
    )(counts, neighbours)


def per_device(features, cotangent, first_weight, second_weight, counts, neighbours):
    needed, lists, pos, parity = tables(counts, neighbours)
    operands = (
        counts,
        lists,
        pos,
        parity,
        features.reshape(PAIRS, 128, 512),
        cotangent.reshape(PAIRS, 128, 512),
        first_weight.transpose(1, 0, 2),
        second_weight.transpose(1, 0, 2),
    )
    out, grads = lax.switch(
        sum((needed[0] > cap).astype(jnp.int32) for cap in CAPS[:-1]),
        [functools.partial(block, cap, i) for i, cap in enumerate(CAPS)],
        *operands,
    )
    return (
        out.reshape(6, 64, 512),
        grads[:, :, :64].astype(F32).transpose(1, 0, 2),
        grads[:, :, 64:].astype(F32).transpose(1, 0, 2),
    )


def solution(mesh):
    placed = (
        P(("group", "dev"), None, None),
        P(("group", "dev"), None, None),
        P(),
        P(),
        P(),
        P(("group", "dev"), None),
    )
    return jax.shard_map(
        per_device,
        mesh=mesh,
        in_specs=placed,
        out_specs=(P(("group", "dev"), None, None), P(), P()),
        check_vma=False,
    )
```
